512 devices in a mesh: replica: 8 (over x, core), mp: 64 (over z, y).
Axes of the slice: x: 4, y: 8, z: 8, core: 2. Of those that a mesh axis runs over, the one named last changes fastest.
Arguments:
- gradient: bfloat16 [8, 4096, 8192], P('replica', 'mp'), may hold values from -6 to 6
- error: bfloat16 [8, 4096, 8192], P('replica', 'mp'), may hold values from -6 to 6
- q_prev: float32 [8192, 64], P('mp'), may hold values from -0.0625 to 0.0625
Outputs:
- new_error: bfloat16 [8, 4096, 8192], P('replica', 'mp')
- q_factor: float32 [8192, 64], P('mp')
- p_factor: float32 [4096, 64], P('mp')
The draws below stay inside these ranges and needn't reach their ends.
All inputs are finite; a program needn't handle non-finite values.
Results may differ from the reference program's by a relative error of at most 0.001.
Values sent between devices are 32-bit elements; how exact they have to be, the bound alone decides.
No kernel may reach another device: no remote copies, remote signals or barrier semaphores. Data moves between devices by JAX's collectives and lax.ppermute only.
A program may use at most 64 MiB of HBM per device.

```python
import jax
import jax.numpy as jnp
from jax import lax

D = 8192
RANK = 64
ROWS = 4096
N_REPLICA = 8


def block_levels(stream_key, dims, shards, low, largest):
    factor_of, own = 1.0, jax.random.fold_in(stream_key, 6)
    for position, blocks in shards:
        heights = jnp.exp(jax.random.uniform(jax.random.fold_in(own, position), (blocks,), jnp.float32, low / len(shards), largest / len(shards)))
        factor_of = factor_of * jnp.repeat(heights, dims[position] // blocks).reshape([-1 if axis == position else 1 for axis in range(len(dims))])
    return factor_of


def gaussian(rng, extent, scale, bound, shards=(), held_as=jnp.bfloat16):
    result = scale * jax.random.normal(rng, extent, jnp.float32)
    if shards:
        result = result * block_levels(rng, extent, shards, -0.22, 0.18)
    return jnp.clip(result, -bound, bound).astype(held_as)


def setup_inputs(seed: int = 0) -> dict:
    streams_of = jax.random.split(jax.random.key(seed), 4)
    gradient = gaussian(streams_of[0], (N_REPLICA, ROWS, D), 1.0, 6.0, ((0, 8), (1, 64)))
    error = gaussian(streams_of[1], (N_REPLICA, ROWS, D), 0.7, 6.0, ((0, 8), (1, 64)))
    q_prev = gaussian(streams_of[2], (D, RANK), D ** -0.5, 0.0625, ((0, 64),), jnp.float32)
    return {"gradient": gradient, "error": error, "q_prev": q_prev}


def reference(gradient, error, q_prev):
    highest = lax.Precision.HIGHEST

    def p_step(total, pair):
        moment = pair[0].astype(jnp.float32) + pair[1].astype(jnp.float32)
        return (total + jnp.dot(moment, q_prev, precision=highest), None)
    p_total, unused = lax.scan(p_step, jnp.zeros((ROWS, RANK), jnp.float32), (gradient, error))
    p_mean = p_total / N_REPLICA
    gram_matrix = jnp.dot(p_mean.T, p_mean, precision=highest)
    lower_factor = jnp.linalg.cholesky(gram_matrix)
    p_factor = lax.linalg.triangular_solve(lower_factor, p_mean, left_side=False, lower=True, transpose_a=True)

    def q_step(total, pair):
        moment = pair[0].astype(jnp.float32) + pair[1].astype(jnp.float32)
        return (total + jnp.dot(moment.T, p_factor, precision=highest), None)
    q_total, unused = lax.scan(q_step, jnp.zeros((D, RANK), jnp.float32), (gradient, error))
    q_factor = q_total / N_REPLICA

    def e_step(pair):
        moment = pair[0].astype(jnp.float32) + pair[1].astype(jnp.float32)
        return (moment - jnp.dot(p_factor, q_factor.T, precision=highest)).astype(jnp.bfloat16)
    new_error = lax.map(e_step, (gradient, error))
    return (new_error, q_factor, p_factor)
```

```python
import functools

import jax
import jax.numpy as jnp
from jax import lax
from jax.experimental import pallas as pl
from jax.experimental.pallas import tpu as pltpu
from jax.sharding import PartitionSpec as P

HIGHEST = lax.Precision.HIGHEST
BLOCK = 128
CORES = 2


def exchange(value, axis, groups=None):
    return lax.all_to_all(value, axis, 0, 0, axis_index_groups=groups)


def spread(value, axis, groups=None):
    count = len(groups[0]) if groups else lax.axis_size(axis)
    return exchange(jnp.broadcast_to(value[None], (count,) + value.shape), axis, groups)


def swap_cores(value, replicas):
    return lax.ppermute(value, "replica", [(r, r ^ 1) for r in range(replicas)])


def fold(square):
    half = square.shape[0] // 2
    return jnp.concatenate([square[:half], square[half:]], axis=1)


def unfold(folded):
    half = folded.shape[1] // 2
    return jnp.concatenate([folded[:, :half], folded[:, half:]], axis=0)


def split_kernel(core_ref, g_keep, e_keep, g_give, e_give, keep, give):
    keep[0] = g_keep[0].astype(jnp.float32) + e_keep[0].astype(jnp.float32)
    give[0] = g_give[0].astype(jnp.float32) + e_give[0].astype(jnp.float32)


def split_moment(core, gradient, error, own):
    _, rows, cols = gradient.shape
    chips = cols // own // CORES
    keep = pl.BlockSpec((1, rows, own), lambda x, core: (0, 0, CORES * x + core[0]))
    give = pl.BlockSpec((1, rows, own), lambda x, core: (0, 0, CORES * x + 1 - core[0]))
    out = pl.BlockSpec((1, rows, own), lambda x, core: (x, 0, 0))
    shape = jax.ShapeDtypeStruct((chips, rows, own), jnp.float32)
    return pl.pallas_call(
        split_kernel,
        grid_spec=pltpu.PrefetchScalarGridSpec(
            num_scalar_prefetch=1, grid=(chips,),
            in_specs=[keep, keep, give, give], out_specs=[out, out]),
        out_shape=[shape, shape],
        cost_estimate=pl.CostEstimate(flops=rows * cols, bytes_accessed=8 * rows * cols, transcendentals=0),
        name="split_moment",
    )(core, gradient, error, gradient, error)


def update_kernel(core_ref, weights, mine, theirs, gradient, error, out):
    core = core_ref[0]
    groups = mine.shape[1]
    own = groups * BLOCK
    factor = weights[...]
    for c in range(CORES):
        for a in range(0, groups, 2):
            right = jnp.concatenate(
                [jnp.where(core == c, mine[0, k], theirs[0, k]) for k in (a, a + 1)], axis=1)
            change = jnp.dot(factor, right, precision=HIGHEST, preferred_element_type=jnp.float32)
            columns = slice(c * own + a * BLOCK, c * own + (a + 2) * BLOCK)
            moment = gradient[0, :, columns].astype(jnp.float32) + error[0, :, columns].astype(jnp.float32)
            out[0, :, columns] = (moment - change).astype(out.dtype)


def update_error(core, weights, mine, theirs, gradient, error):
    _, rows, cols = gradient.shape
    chips, groups, rank, _ = mine.shape
    wide = cols // chips
    whole = pl.BlockSpec(weights.shape, lambda x, core: (0, 0))
    chunk = pl.BlockSpec((1, groups, rank, BLOCK), lambda x, core: (x, 0, 0, 0))
    band = pl.BlockSpec((1, rows, wide), lambda x, core: (0, 0, x))
    return pl.pallas_call(
        update_kernel,
        grid_spec=pltpu.PrefetchScalarGridSpec(
            num_scalar_prefetch=1, grid=(chips,),
            in_specs=[whole, chunk, chunk, band, band], out_specs=band),
        out_shape=jax.ShapeDtypeStruct(gradient.shape, gradient.dtype),
        cost_estimate=pl.CostEstimate(
            flops=2 * rows * cols * rank, bytes_accessed=6 * rows * cols + 4 * rank * cols, transcendentals=0),
        name="update_error",
    )(core, weights, mine, theirs, gradient, error)


def body(gradient, error, q_prev):
    replicas = lax.axis_size("replica")
    shards = lax.axis_size("mp")
    rows, cols = gradient.shape[1:]
    rank = q_prev.shape[1]
    own = cols // replicas
    groups = own // BLOCK
    slab = rank // replicas
    replica = lax.axis_index("replica")
    shard = lax.axis_index("mp")
    core = lax.rem(replica, CORES)
    core_arg = core.astype(jnp.int32).reshape(1)
    chip_groups = [[c + CORES * x for x in range(replicas // CORES)] for c in range(CORES)]
    inner_groups = [[o * replicas + i for i in range(replicas)] for o in range(groups)]
    outer_groups = [[o * replicas + i for o in range(groups)] for i in range(replicas)]

    pairs = [
        (b * shards + r * groups + a, r * shards + a * replicas + b)
        for r in range(replicas) for a in range(groups) for b in range(replicas)
    ]
    tile = lax.dynamic_slice_in_dim(q_prev.T, replica * slab, slab, 0)
    tile = lax.ppermute(tile, ("replica", "mp"), pairs)
    q_block = spread(tile, "mp", inner_groups).reshape(rank, BLOCK)
    q_blocks = spread(q_block, "mp", outer_groups)
    q_own = q_blocks.transpose(1, 0, 2).reshape(rank, own)

    keep, give = split_moment(core_arg, gradient, error, own)
    pair_sum = keep + swap_cores(give, replicas)
    mean = exchange(pair_sum, "replica", chip_groups).sum(0) / replicas

    p_part = lax.dot_general(mean, q_own, (((1,), (1,)), ((), ())), precision=HIGHEST)
    p_mean = unfold(spread(fold(p_part), "replica").sum(0))

    s_part = lax.dot_general(p_mean, mean, (((0,), (0,)), ((), ())), precision=HIGHEST)
    s_part = s_part.reshape(replicas, slab, groups, BLOCK).transpose(2, 0, 1, 3)
    s_tile = exchange(s_part.reshape(shards, slab, BLOCK), "mp").sum(0)
    s_blocks = spread(s_tile, "mp").reshape(groups, rank, BLOCK)
    s_own = s_blocks.transpose(1, 0, 2).reshape(rank, own)
    gram_part = lax.dot_general(s_own, q_own, (((1,), (1,)), ((), ())), precision=HIGHEST)
    gram = unfold(spread(fold(gram_part), "replica").sum(0))
    mine = spread(s_blocks, "replica", chip_groups)
    theirs = swap_cores(mine, replicas)

    lower = jnp.linalg.cholesky(gram)
    p_factor = lax.linalg.triangular_solve(
        lower, p_mean, left_side=False, lower=True, transpose_a=True
    )
    weights = lax.linalg.triangular_solve(lower, p_factor, left_side=False, lower=True)
    owner, block = shard // groups, lax.rem(shard, groups)
    start = (owner // CORES, block, 0, 0)
    sizes = (1, 1, rank, BLOCK)
    s_block = jnp.where(
        lax.rem(owner, CORES) == core,
        lax.dynamic_slice(mine, start, sizes), lax.dynamic_slice(theirs, start, sizes))[0, 0]
    q_factor = lax.linalg.triangular_solve(lower, s_block, left_side=True, lower=True).T
    new_error = update_error(core_arg, weights, mine, theirs, gradient, error)
    return (new_error, q_factor, p_factor)


def solution(mesh):
    return jax.shard_map(
        body,
        mesh=mesh,
        in_specs=(P("replica", "mp", None), P("replica", "mp", None), P("mp", None)),
        out_specs=(P("replica", "mp", None), P("mp", None), P("mp", None)),
        check_vma=False,
    )
```

```python
import jax
import jax.numpy as jnp
from jax import lax
from jax.experimental import pallas as pl
from jax.experimental.pallas import tpu as pltpu
from jax.sharding import PartitionSpec as P

HIGHEST = lax.Precision.HIGHEST
BLOCK = 128
CORES = 2
SLAB = 16


def exchange(value, axis, groups=None):
    return lax.all_to_all(value, axis, 0, 0, axis_index_groups=groups)


def spread(value, axis, groups=None):
    count = len(groups[0]) if groups else lax.axis_size(axis)
    return exchange(jnp.broadcast_to(value[None], (count,) + value.shape), axis, groups)


def swap_cores(value, replicas):
    return lax.ppermute(value, "replica", [(r, r ^ 1) for r in range(replicas)])


def fold(square):
    half = square.shape[0] // 2
    return jnp.concatenate([square[:half], square[half:]], axis=1)


def unfold(folded):
    half = folded.shape[1] // 2
    return jnp.concatenate([folded[:, :half], folded[:, half:]], axis=0)


def own_columns(ref, chunk, k, stride):
    return ref[0, :, pl.ds(pl.multiple_of((k * stride + chunk) * BLOCK, BLOCK), BLOCK)]


def give_kernel(core_ref, gradient, error, give):
    chips, _, own = give.shape
    for x in range(chips):
        chunk = CORES * x + 1 - core_ref[0]
        for k in range(own // BLOCK):
            g, e = (own_columns(ref, chunk, k, CORES * chips) for ref in (gradient, error))
            give[x, :, k * BLOCK:(k + 1) * BLOCK] = g.astype(jnp.float32) + e.astype(jnp.float32)


def keep_kernel(core_ref, gradient, error, came, total):
    chips, _, own = total.shape
    for x in range(chips):
        chunk = CORES * x + core_ref[0]
        for k in range(own // BLOCK):
            g, e = (own_columns(ref, chunk, k, CORES * chips) for ref in (gradient, error))
            columns = slice(k * BLOCK, (k + 1) * BLOCK)
            moment = g.astype(jnp.float32) + e.astype(jnp.float32)
            total[x, :, columns] = moment + came[x, :, columns]


def moment_chunks(kernel, core, gradient, error, own, came=()):
    _, rows, cols = gradient.shape
    chips = cols // own // CORES
    band = pl.BlockSpec((1, SLAB, cols), lambda i, core: (0, i, 0))
    part = pl.BlockSpec((chips, SLAB, own), lambda i, core: (0, i, 0))
    return pl.pallas_call(
        kernel,
        grid_spec=pltpu.PrefetchScalarGridSpec(
            num_scalar_prefetch=1, grid=(rows // SLAB,),
            in_specs=[band, band] + [part] * len(came), out_specs=part),
        out_shape=jax.ShapeDtypeStruct((chips, rows, own), jnp.float32),
        cost_estimate=pl.CostEstimate(flops=rows * cols, bytes_accessed=6 * rows * cols, transcendentals=0),
        name="moment_chunks",
    )(core, gradient, error, *came)


def update_kernel(place, weights, inverse, mine, theirs, gradient, error, out, right):
    chips, _, rank, _ = mine.shape
    core, block, chip, parity = (place[i] for i in range(4))
    factor = weights[...]
    high = factor.astype(jnp.bfloat16).astype(jnp.float32)
    lane = lax.broadcasted_iota(jnp.int32, factor.shape, 1)
    factor = jnp.where(lane < 2 * rank, high, factor - high).astype(jnp.bfloat16)
    for x in range(chips):
        own, other = mine[x, 0], theirs[x, 0]
        s = jnp.concatenate([jnp.where(core == 0, own, other), jnp.where(core == 0, other, own)], axis=1)
        s_high = s.astype(jnp.bfloat16)
        s_low = (s - s_high.astype(jnp.float32)).astype(jnp.bfloat16)
        stack = jnp.concatenate([s_high, s_low, s_high, s_low], axis=0)
        change = jnp.dot(factor, stack, preferred_element_type=jnp.float32)
        columns = slice(CORES * x * BLOCK, CORES * (x + 1) * BLOCK)
        moment = gradient[0, :, columns].astype(jnp.float32) + error[0, :, columns].astype(jnp.float32)
        out[0, :, columns] = (moment - change).astype(out.dtype)

    @pl.when(pl.program_id(0) == block)
    def _():
        s = jnp.where(core == parity, mine[chip, 0], theirs[chip, 0])
        right[...] = jnp.dot(inverse[...], s, precision=HIGHEST, preferred_element_type=jnp.float32)


def update_error(place, weights, inverse, mine, theirs, gradient, error):
    _, rows, cols = gradient.shape
    chips, groups, rank, _ = mine.shape
    factor = pl.BlockSpec(weights.shape, lambda a, place: (0, 0))
    lower = pl.BlockSpec(inverse.shape, lambda a, place: (0, 0))
    tiles = pl.BlockSpec((chips, 1, rank, BLOCK), lambda a, place: (0, a, 0, 0))
    band = pl.BlockSpec((1, rows, cols // groups), lambda a, place: (0, 0, a))
    right = pl.BlockSpec((rank, BLOCK), lambda a, place: (0, 0))
    return pl.pallas_call(
        update_kernel,
        grid_spec=pltpu.PrefetchScalarGridSpec(
            num_scalar_prefetch=1, grid=(groups,),
            in_specs=[factor, lower, tiles, tiles, band, band], out_specs=[band, right]),
        out_shape=[jax.ShapeDtypeStruct(gradient.shape, gradient.dtype),
                   jax.ShapeDtypeStruct((rank, BLOCK), jnp.float32)],
        cost_estimate=pl.CostEstimate(
            flops=8 * rows * cols * rank, bytes_accessed=6 * rows * cols + 4 * rank * cols, transcendentals=0),
        name="update_error",
    )(place, weights, inverse, mine, theirs, gradient, error)


def unpack_kernel(tiles, copies, gram):
    count, groups, rank, _ = copies.shape
    slab = tiles.shape[1] // 2
    for a in range(groups):
        for b in range(rank // slab):
            tile = tiles[a * (rank // slab) + b, :slab]
            for x in range(count):
                copies[x, a, b * slab:(b + 1) * slab] = tile
    gram[...] = tiles[:, slab][:, :rank]


def unpack(tiles, count, groups, rank):
    return pl.pallas_call(
        unpack_kernel,
        out_shape=[jax.ShapeDtypeStruct((count, groups, rank, BLOCK), jnp.float32),
                   jax.ShapeDtypeStruct((rank, rank), jnp.float32)],
        cost_estimate=pl.CostEstimate(flops=0, bytes_accessed=tiles.size * 12, transcendentals=0),
        name="unpack",
    )(tiles)


def body(gradient, error, q_prev):
    replicas = lax.axis_size("replica")
    shards = lax.axis_size("mp")
    rows, cols = gradient.shape[1:]
    rank = q_prev.shape[1]
    own = cols // replicas
    groups = own // BLOCK
    slab = rank // replicas
    replica = lax.axis_index("replica").astype(jnp.int32)
    shard = lax.axis_index("mp").astype(jnp.int32)
    core = replica % CORES
    outer, inner = shard // replicas, shard % replicas
    chip_groups = [[c + CORES * x for x in range(replicas // CORES)] for c in range(CORES)]
    outer_groups = [[o * replicas + i for o in range(groups)] for i in range(replicas)]

    q_near = spread(q_prev.T, "mp", outer_groups)

    core_arg = core.reshape(1)
    give = moment_chunks(give_kernel, core_arg, gradient, error, own)
    came = swap_cores(give, replicas)
    total = moment_chunks(keep_kernel, core_arg, gradient, error, own, (came,))
    q_near, total = lax.optimization_barrier((q_near, total))
    q_blocks = lax.ppermute(q_near, ("replica", "mp"), [
        (r * shards + o * replicas + i, i * shards + o * replicas + r)
        for r in range(replicas) for o in range(groups) for i in range(replicas)
    ])
    q_own = q_blocks.transpose(1, 0, 2).reshape(rank, own)
    mean = exchange(total, "replica", chip_groups).sum(0) / replicas

    p_part = lax.dot_general(mean, q_own, (((1,), (1,)), ((), ())), precision=HIGHEST)
    p_mean = unfold(spread(fold(p_part), "replica").sum(0))

    s_part = lax.dot_general(p_mean, mean, (((0,), (0,)), ((), ())), precision=HIGHEST)
    s_part = s_part.reshape(replicas, slab, groups, BLOCK).transpose(2, 0, 1, 3)
    gram_part = lax.dot_general(p_mean, p_mean, (((0,), (0,)), ((), ())), precision=HIGHEST)
    gram_part = jnp.pad(gram_part[:, None], ((0, 0), (0, slab - 1), (0, BLOCK - rank)))
    tiles = jnp.concatenate([s_part.reshape(shards, slab, BLOCK), gram_part], axis=1)
    tiles = spread(exchange(tiles, "mp").sum(0), "mp")
    copies, gram = unpack(tiles, replicas // CORES, groups, rank)
    mine = exchange(copies, "replica", chip_groups)

    lower = jnp.linalg.cholesky(gram)
    inverse = lax.linalg.triangular_solve(
        lower, jnp.eye(rank, dtype=jnp.float32), left_side=True, lower=True
    )
    p_factor = lax.dot_general(p_mean, inverse, (((1,), (1,)), ((), ())), precision=HIGHEST)
    weights = jnp.dot(p_factor, inverse, precision=HIGHEST)
    weights = jnp.tile(weights, (1, 4))
    mine, weights, inverse = lax.optimization_barrier((mine, weights, inverse))
    theirs = swap_cores(mine, replicas)

    place = jnp.stack([core, outer, inner // CORES, inner % CORES])
    new_error, right = update_error(place, weights, inverse, mine, theirs, gradient, error)
    return (new_error, right.T, p_factor)


def solution(mesh):
    return jax.shard_map(
        body,
        mesh=mesh,
        in_specs=(P("replica", "mp", None), P("replica", "mp", None), P("mp", None)),
        out_specs=(P("replica", "mp", None), P("mp", None), P("mp", None)),
        check_vma=False,
    )
```

```python
import jax
import jax.numpy as jnp
from jax import lax
from jax.experimental import pallas as pl
from jax.experimental.pallas import tpu as pltpu
from jax.sharding import PartitionSpec as P

HIGHEST = lax.Precision.HIGHEST
BLOCK = 128
CORES = 2
SLAB = 16
TILE = 8
PACK = 9
PARAMS = pltpu.CompilerParams(vmem_limit_bytes=16 * 2**20)


def exchange(value, axis, groups=None):
    return lax.all_to_all(value, axis, 0, 0, axis_index_groups=groups)


def swap_cores(value, replicas):
    return lax.ppermute(value, "replica", [(r, r ^ 1) for r in range(replicas)])


def split_kernel(core_ref, gradient, error, keep, give):
    chips, _, own = keep.shape
    for x in range(chips):
        for out, core in ((keep, core_ref[0]), (give, 1 - core_ref[0])):
            for k in range(own // BLOCK):
                start = pl.multiple_of((k * CORES * chips + CORES * x + core) * BLOCK, BLOCK)
                g, e = (ref[0, :, pl.ds(start, BLOCK)].astype(jnp.float32) for ref in (gradient, error))
                out[x, :, k * BLOCK:(k + 1) * BLOCK] = g + e


def split_moment(core, gradient, error, own):
    _, rows, cols = gradient.shape
    chips = cols // own // CORES
    band = pl.BlockSpec((1, SLAB, cols), lambda i, core: (0, i, 0))
    part = pl.BlockSpec((chips, SLAB, own), lambda i, core: (0, i, 0))
    shape = jax.ShapeDtypeStruct((chips, rows, own), jnp.float32)
    return pl.pallas_call(
        split_kernel,
        grid_spec=pltpu.PrefetchScalarGridSpec(
            num_scalar_prefetch=1, grid=(rows // SLAB,), in_specs=[band, band], out_specs=[part, part]),
        out_shape=[shape, shape],
        cost_estimate=pl.CostEstimate(flops=rows * cols, bytes_accessed=8 * rows * cols, transcendentals=0),
        compiler_params=PARAMS,
        name="split_moment",
    )(core, gradient, error)


def product_kernel(outer_ref, parts, *refs):
    *lists, mean, copies, q_list = refs
    mean[...] = (parts[0] + parts[1] + parts[2] + parts[3]) * (1.0 / copies.shape[0])
    near = lists[0].shape[0]
    for i, piece in enumerate(lists):
        q_list[i * near:(i + 1) * near] = piece[...]
    blocks = []
    for a in range(q_list.shape[0]):
        apart = outer_ref[0] ^ a
        blocks.append(q_list[((apart & 3) << 1) | (apart >> 2)])
    q_own = jnp.concatenate(blocks, axis=1)
    p = lax.dot_general(mean[...], q_own, (((1,), (1,)), ((), ())), precision=HIGHEST,
                        preferred_element_type=jnp.float32)
    half = p.shape[0] // 2
    folded = jnp.concatenate([p[:half], p[half:]], axis=1)
    for r in range(copies.shape[0]):
        copies[r] = folded


def product(outer, parts, lists, replicas):
    _, rows, own = parts.shape
    near, rank, _ = lists[0].shape
    full = lambda *shape: pl.BlockSpec(shape, lambda i, outer: (0,) * len(shape))
    return pl.pallas_call(
        product_kernel,
        grid_spec=pltpu.PrefetchScalarGridSpec(
            num_scalar_prefetch=1, grid=(1,),
            in_specs=[full(*parts.shape)] + [full(*piece.shape) for piece in lists],
            out_specs=[full(rows, own), full(replicas, rows // 2, 2 * rank)],
            scratch_shapes=[pltpu.VMEM((near * len(lists), rank, BLOCK), jnp.float32)]),
        out_shape=[jax.ShapeDtypeStruct((rows, own), jnp.float32),
                   jax.ShapeDtypeStruct((replicas, rows // 2, 2 * rank), jnp.float32)],
        cost_estimate=pl.CostEstimate(flops=2 * rows * own * rank, bytes_accessed=4 * parts.size, transcendentals=0),
        compiler_params=PARAMS,
        name="product",
    )(outer, parts, *lists)


def pack_kernel(p_parts, mean, p_mean, tiles):
    folded = p_parts[0]
    for r in range(1, p_parts.shape[0]):
        folded = folded + p_parts[r]
    rank = folded.shape[1] // 2
    p = jnp.concatenate([folded[:, :rank], folded[:, rank:]], axis=0)
    p_mean[...] = p
    over_rows = (((0,), (0,)), ((), ()))
    s = lax.dot_general(p, mean[...], over_rows, precision=HIGHEST, preferred_element_type=jnp.float32)
    gram = lax.dot_general(p, p, over_rows, precision=HIGHEST, preferred_element_type=jnp.float32)
    gram = jnp.concatenate([gram] * (BLOCK // rank), axis=1)
    slabs = rank // TILE
    for a in range(mean.shape[1] // BLOCK):
        for b in range(slabs):
            t = a * slabs + b
            tiles[t * PACK:t * PACK + TILE] = s[b * TILE:(b + 1) * TILE, a * BLOCK:(a + 1) * BLOCK]
            tiles[t * PACK + TILE:(t + 1) * PACK] = gram[t:t + 1]


def pack(p_parts, mean, shards):
    rows, own = mean.shape
    rank = p_parts.shape[2] // 2
    return pl.pallas_call(
        pack_kernel,
        out_shape=[jax.ShapeDtypeStruct((rows, rank), jnp.float32),
                   jax.ShapeDtypeStruct((shards * PACK, BLOCK), jnp.float32)],
        cost_estimate=pl.CostEstimate(flops=2 * rows * own * rank, bytes_accessed=8 * mean.size, transcendentals=0),
        compiler_params=PARAMS,
        name="pack",
    )(p_parts, mean)


def total_kernel(tiles, copies):
    shards = tiles.shape[0] // PACK
    parts = [tiles[t * PACK:(t + 1) * PACK] for t in range(shards)]
    while len(parts) > 1:
        parts = [parts[i] + parts[i + 1] for i in range(0, len(parts), 2)]
    for t in range(shards):
        copies[t * PACK:(t + 1) * PACK] = parts[0]


def total(tiles):
    return pl.pallas_call(
        total_kernel,
        out_shape=jax.ShapeDtypeStruct(tiles.shape, tiles.dtype),
        cost_estimate=pl.CostEstimate(flops=tiles.size, bytes_accessed=8 * tiles.size, transcendentals=0),
        compiler_params=PARAMS,
        name="total",
    )(tiles)


def unpack_kernel(tiles, copies, gram):
    count, groups, rank, _ = copies.shape
    slabs = rank // TILE
    for a in range(groups):
        for b in range(slabs):
            t = a * slabs + b
            tile = tiles[t * PACK:t * PACK + TILE]
            for x in range(count):
                copies[x, a, b * TILE:(b + 1) * TILE] = tile
            gram[t:t + 1] = tiles[t * PACK + TILE:(t + 1) * PACK, :rank]


def unpack(tiles, count, groups, rank):
    return pl.pallas_call(
        unpack_kernel,
        out_shape=[jax.ShapeDtypeStruct((count, groups, rank, BLOCK), jnp.float32),
                   jax.ShapeDtypeStruct((rank, rank), jnp.float32)],
        cost_estimate=pl.CostEstimate(flops=0, bytes_accessed=tiles.size * 20, transcendentals=0),
        compiler_params=PARAMS,
        name="unpack",
    )(tiles)


def factors_kernel(p_mean, inverse, p_factor, weights):
    p = lax.dot_general(p_mean[...], inverse[...], (((1,), (1,)), ((), ())), precision=HIGHEST,
                        preferred_element_type=jnp.float32)
    w = jnp.dot(p, inverse[...], precision=HIGHEST, preferred_element_type=jnp.float32)
    p_factor[...] = p
    weights[...] = jnp.concatenate([w, w], axis=1)


def factors(p_mean, inverse):
    rows, rank = p_mean.shape
    return pl.pallas_call(
        factors_kernel,
        out_shape=[jax.ShapeDtypeStruct((rows, rank), jnp.float32),
                   jax.ShapeDtypeStruct((rows, 2 * rank), jnp.float32)],
        cost_estimate=pl.CostEstimate(flops=4 * rows * rank * rank, bytes_accessed=20 * rows * rank, transcendentals=0),
        compiler_params=PARAMS,
        name="factors",
    )(p_mean, inverse)


def update_kernel(place, weights, inverse, mine, theirs, gradient, error, out, right):
    chips, blocks, rank, _ = mine.shape
    core, block, chip, parity = (place[i] for i in range(4))
    high = weights[...].astype(jnp.bfloat16)
    low = (weights[...] - high.astype(jnp.float32)).astype(jnp.bfloat16)
    factor = jnp.concatenate([high, low], axis=0)
    rows = high.shape[0]
    for a in range(blocks):
        for x in range(chips):
            own, other = mine[x, a], theirs[x, a]
            s = jnp.concatenate([jnp.where(core == 0, own, other), jnp.where(core == 0, other, own)], axis=1)
            s_high = s.astype(jnp.bfloat16)
            s_low = (s - s_high.astype(jnp.float32)).astype(jnp.bfloat16)
            stack = jnp.concatenate([s_high, s_low], axis=0)
            change = jnp.dot(factor, stack, preferred_element_type=jnp.float32)
            start = CORES * (a * chips + x) * BLOCK
            columns = slice(start, start + CORES * BLOCK)
            moment = gradient[0, :, columns].astype(jnp.float32) + error[0, :, columns].astype(jnp.float32)
            out[0, :, columns] = (moment - (change[:rows] + change[rows:])).astype(out.dtype)

    @pl.when(pl.program_id(0) == block // blocks)
    def _():
        within = block % blocks
        s = jnp.where(core == parity, mine[chip, within], theirs[chip, within])
        right[...] = jnp.dot(inverse[...], s, precision=HIGHEST, preferred_element_type=jnp.float32)


def update_error(place, weights, inverse, mine, theirs, gradient, error):
    _, rows, cols = gradient.shape
    chips, groups, rank, _ = mine.shape
    steps = 4
    factor = pl.BlockSpec(weights.shape, lambda a, place: (0, 0))
    lower = pl.BlockSpec(inverse.shape, lambda a, place: (0, 0))
    tiles = pl.BlockSpec((chips, groups // steps, rank, BLOCK), lambda a, place: (0, a, 0, 0))
    band = pl.BlockSpec((1, rows, cols // steps), lambda a, place: (0, 0, a))
    right = pl.BlockSpec((rank, BLOCK), lambda a, place: (0, 0))
    return pl.pallas_call(
        update_kernel,
        grid_spec=pltpu.PrefetchScalarGridSpec(
            num_scalar_prefetch=1, grid=(steps,),
            in_specs=[factor, lower, tiles, tiles, band, band], out_specs=[band, right]),
        out_shape=[jax.ShapeDtypeStruct(gradient.shape, gradient.dtype),
                   jax.ShapeDtypeStruct((rank, BLOCK), jnp.float32)],
        cost_estimate=pl.CostEstimate(
            flops=8 * rows * cols * rank, bytes_accessed=6 * rows * cols + 8 * rank * cols, transcendentals=0),
        compiler_params=PARAMS,
        name="update_error",
    )(place, weights, inverse, mine, theirs, gradient, error)


def body(gradient, error, q_prev):
    replicas = lax.axis_size("replica")
    shards = lax.axis_size("mp")
    rows, cols = gradient.shape[1:]
    rank = q_prev.shape[1]
    own = cols // replicas
    groups = own // BLOCK
    replica = lax.axis_index("replica").astype(jnp.int32)
    shard = lax.axis_index("mp").astype(jnp.int32)
    core = replica % CORES
    outer, inner = shard // replicas, shard % replicas
    chip_groups = [[c + CORES * x for x in range(replicas // CORES)] for c in range(CORES)]

    def along(apart):
        return [(r * shards + o * replicas + i, i * shards + (o ^ apart) * replicas + r)
                for r in range(replicas) for o in range(groups) for i in range(replicas)]
    near = [lax.ppermute(q_prev.T[None], ("replica", "mp"), along(apart)) for apart in (0, 4)]

    keep, give = split_moment(core.reshape(1), gradient, error, own)
    paired, near = lax.optimization_barrier((keep + swap_cores(give, replicas), jnp.concatenate(near, axis=0)))
    parts = exchange(paired, "replica", chip_groups)
    lists = [near] + [
        lax.ppermute(near, "mp", [(j, j ^ (apart * replicas)) for j in range(shards)]) for apart in (1, 2, 3)]
    mean, copies = product(outer.reshape(1), parts, lists, replicas)

    p_mean, tiles = pack(exchange(copies, "replica"), mean, shards)
    packed = (shards, PACK, 1, BLOCK)
    tiles = exchange(tiles.reshape(packed), "mp").reshape(tiles.shape)
    tiles = exchange(total(tiles).reshape(packed), "mp").reshape(tiles.shape)
    copies, gram = unpack(tiles, replicas // CORES, groups, rank)
    mine = exchange(copies, "replica", chip_groups)

    lower = jnp.linalg.cholesky(gram)
    inverse = lax.linalg.triangular_solve(
        lower, jnp.eye(rank, dtype=jnp.float32), left_side=True, lower=True
    )
    p_factor, weights = factors(p_mean, inverse)
    mine, weights, inverse = lax.optimization_barrier((mine, weights, inverse))
    theirs = swap_cores(mine, replicas)

    place = jnp.stack([core, outer, inner // CORES, inner % CORES])
    new_error, right = update_error(place, weights, inverse, mine, theirs, gradient, error)
    return (new_error, right.T, p_factor)


def solution(mesh):
    return jax.shard_map(
        body,
        mesh=mesh,
        in_specs=(P("replica", "mp", None), P("replica", "mp", None), P("mp", None)),
        out_specs=(P("replica", "mp", None), P("mp", None), P("mp", None)),
        check_vma=False,
    )
```

```python
import jax
import jax.numpy as jnp
from jax import lax
from jax.experimental import pallas as pl
from jax.experimental.pallas import tpu as pltpu
from jax.sharding import PartitionSpec as P

HIGHEST = lax.Precision.HIGHEST
BLOCK = 128
CORES = 2
TILE = 8
PACK = 9
PARAMS = pltpu.CompilerParams(vmem_limit_bytes=16 * 2**20)


def exchange(value, axis, groups=None):
    return lax.all_to_all(value, axis, 0, 0, axis_index_groups=groups)


def swap_cores(value, replicas):
    return lax.ppermute(value, "replica", [(r, r ^ 1) for r in range(replicas)])


SCALARS = pl.BlockSpec(memory_space=pltpu.SMEM)
VECTORS = pl.BlockSpec(memory_space=pltpu.VMEM)


def moment_block(gradient, error, block):
    columns = pl.ds(pl.multiple_of(block * BLOCK, BLOCK), BLOCK)
    return gradient[0, :, columns].astype(jnp.float32) + error[0, :, columns].astype(jnp.float32)


def split_kernel(core_ref, gradient, error, keep, give):
    chips, _, own = keep.shape
    for x in range(chips):
        for out, core in ((keep, core_ref[0]), (give, 1 - core_ref[0])):
            for k in range(own // BLOCK):
                out[x, :, k * BLOCK:(k + 1) * BLOCK] = moment_block(
                    gradient, error, CORES * (k * chips + x) + core)


def split_moment(core, gradient, error, own):
    _, rows, cols = gradient.shape
    shape = jax.ShapeDtypeStruct((cols // own // CORES, rows, own), jnp.float32)
    return pl.pallas_call(
        split_kernel,
        in_specs=[SCALARS, VECTORS, VECTORS],
        out_shape=[shape, shape],
        cost_estimate=pl.CostEstimate(flops=rows * cols, bytes_accessed=8 * rows * cols, transcendentals=0),
        compiler_params=PARAMS,
        name="split_moment",
    )(core, gradient, error)


def product_kernel(outer_ref, parts, *refs):
    *blocks, mean, copies, q_list = refs
    mean[...] = (parts[0] + parts[1] + parts[2] + parts[3]) * (1.0 / copies.shape[0])
    for apart, block in enumerate(blocks):
        q_list[apart] = block[...]
    q_own = jnp.concatenate([q_list[outer_ref[0] ^ a] for a in range(len(blocks))], axis=1)
    p = lax.dot_general(mean[...], q_own, (((1,), (1,)), ((), ())), precision=HIGHEST,
                        preferred_element_type=jnp.float32)
    half = p.shape[0] // 2
    folded = jnp.concatenate([p[:half], p[half:]], axis=1)
    for r in range(copies.shape[0]):
        copies[r] = folded


def product(outer, parts, blocks, replicas):
    _, rows, own = parts.shape
    rank = blocks[0].shape[0]
    return pl.pallas_call(
        product_kernel,
        in_specs=[SCALARS, VECTORS] + [VECTORS] * len(blocks),
        out_shape=[jax.ShapeDtypeStruct((rows, own), jnp.float32),
                   jax.ShapeDtypeStruct((replicas, rows // 2, 2 * rank), jnp.float32)],
        scratch_shapes=[pltpu.VMEM((len(blocks), rank, BLOCK), jnp.float32)],
        cost_estimate=pl.CostEstimate(flops=2 * rows * own * rank, bytes_accessed=4 * parts.size, transcendentals=0),
        compiler_params=PARAMS,
        name="product",
    )(outer, parts, *blocks)


def pack_kernel(p_parts, mean, p_mean, tiles):
    folded = p_parts[0]
    for r in range(1, p_parts.shape[0]):
        folded = folded + p_parts[r]
    rank = folded.shape[1] // 2
    p = jnp.concatenate([folded[:, :rank], folded[:, rank:]], axis=0)
    p_mean[...] = p
    over_rows = (((0,), (0,)), ((), ()))
    s = lax.dot_general(p, mean[...], over_rows, precision=HIGHEST, preferred_element_type=jnp.float32)
    gram = lax.dot_general(p, p, over_rows, precision=HIGHEST, preferred_element_type=jnp.float32)
    gram = jnp.concatenate([gram] * (BLOCK // rank), axis=1)
    slabs = rank // TILE
    for a in range(mean.shape[1] // BLOCK):
        for b in range(slabs):
            t = a * slabs + b
            tiles[t * PACK:t * PACK + TILE] = s[b * TILE:(b + 1) * TILE, a * BLOCK:(a + 1) * BLOCK]
            tiles[t * PACK + TILE:(t + 1) * PACK] = gram[t:t + 1]


def pack(p_parts, mean, shards):
    rows, own = mean.shape
    rank = p_parts.shape[2] // 2
    return pl.pallas_call(
        pack_kernel,
        out_shape=[jax.ShapeDtypeStruct((rows, rank), jnp.float32),
                   jax.ShapeDtypeStruct((shards * PACK, BLOCK), jnp.float32)],
        cost_estimate=pl.CostEstimate(flops=2 * rows * own * rank, bytes_accessed=8 * mean.size, transcendentals=0),
        compiler_params=PARAMS,
        name="pack",
    )(p_parts, mean)


def total_kernel(tiles, copies):
    shards = tiles.shape[0] // PACK
    parts = [tiles[t * PACK:(t + 1) * PACK] for t in range(shards)]
    while len(parts) > 1:
        parts = [parts[i] + parts[i + 1] for i in range(0, len(parts), 2)]
    for t in range(shards):
        copies[t * PACK:(t + 1) * PACK] = parts[0]


def total(tiles):
    return pl.pallas_call(
        total_kernel,
        out_shape=jax.ShapeDtypeStruct(tiles.shape, tiles.dtype),
        cost_estimate=pl.CostEstimate(flops=tiles.size, bytes_accessed=8 * tiles.size, transcendentals=0),
        compiler_params=PARAMS,
        name="total",
    )(tiles)


def unpack_kernel(tiles, copies, gram):
    count, groups, rank, _ = copies.shape
    slabs = rank // TILE
    for a in range(groups):
        for b in range(slabs):
            t = a * slabs + b
            tile = tiles[t * PACK:t * PACK + TILE]
            for x in range(count):
                copies[x, a, b * TILE:(b + 1) * TILE] = tile
            gram[t:t + 1] = tiles[t * PACK + TILE:(t + 1) * PACK, :rank]


def unpack(tiles, count, groups, rank):
    return pl.pallas_call(
        unpack_kernel,
        out_shape=[jax.ShapeDtypeStruct((count, groups, rank, BLOCK), jnp.float32),
                   jax.ShapeDtypeStruct((rank, rank), jnp.float32)],
        cost_estimate=pl.CostEstimate(flops=0, bytes_accessed=tiles.size * 20, transcendentals=0),
        compiler_params=PARAMS,
        name="unpack",
    )(tiles)


def factors_kernel(p_mean, inverse, p_factor, weights):
    p = lax.dot_general(p_mean[...], inverse[...], (((1,), (1,)), ((), ())), precision=HIGHEST,
                        preferred_element_type=jnp.float32)
    w = jnp.dot(p, inverse[...], precision=HIGHEST, preferred_element_type=jnp.float32)
    p_factor[...] = p
    weights[...] = jnp.concatenate([w, w], axis=1)


def factors(p_mean, inverse):
    rows, rank = p_mean.shape
    return pl.pallas_call(
        factors_kernel,
        out_shape=[jax.ShapeDtypeStruct((rows, rank), jnp.float32),
                   jax.ShapeDtypeStruct((rows, 2 * rank), jnp.float32)],
        cost_estimate=pl.CostEstimate(flops=4 * rows * rank * rank, bytes_accessed=20 * rows * rank, transcendentals=0),
        compiler_params=PARAMS,
        name="factors",
    )(p_mean, inverse)


def halves(value, axis):
    high = value.astype(jnp.bfloat16)
    low = (value - high.astype(jnp.float32)).astype(jnp.bfloat16)
    return jnp.concatenate([high, low], axis=axis)


def remainder(factor, s, x, a, core, gradient, error):
    chips, _, rank, _ = s.shape
    stack = halves(jnp.concatenate([s[x, a], s[x + 1, a]], axis=1), 0)
    change = jnp.dot(factor, stack, preferred_element_type=jnp.float32)
    rows = change.shape[0] // 2
    change = change[:rows] + change[rows:]
    return [
        (moment_block(gradient, error, CORES * (a * chips + x + i) + core)
         - change[:, i * BLOCK:(i + 1) * BLOCK]).astype(gradient.dtype)
        for i in range(2)]


def near_kernel(place, weights, mine, gradient, error, out):
    chips, groups, _, _ = mine.shape
    factor = halves(weights[...], 0)
    for a in range(groups):
        for x in range(0, chips, 2):
            out[x, a], out[x + 1, a] = remainder(factor, mine, x, a, place[0], gradient, error)


def update_near(place, weights, mine, gradient, error):
    _, rows, cols = gradient.shape
    chips, groups, rank, _ = mine.shape
    return pl.pallas_call(
        near_kernel,
        in_specs=[SCALARS] + [VECTORS] * 4,
        out_shape=jax.ShapeDtypeStruct((chips, groups, rows, BLOCK), gradient.dtype),
        cost_estimate=pl.CostEstimate(
            flops=4 * rows * cols * rank, bytes_accessed=4 * rows * cols, transcendentals=0),
        compiler_params=PARAMS,
        name="update_near",
    )(place, weights, mine, gradient, error)


def far_kernel(place, weights, inverse, mine, theirs, near, gradient, error, out, right, bands, done):
    chips, groups, _, _ = mine.shape
    core, block, chip, parity = (place[i] for i in range(4))
    factor = halves(weights[...], 0)
    copies = []
    for a in range(groups):
        for x in range(0, chips, 2):
            far = remainder(factor, theirs, x, a, 1 - core, gradient, error)
            for i in range(2):
                for value, owner in ((near[x + i, a], core), (far[i], 1 - core)):
                    start = pl.multiple_of((CORES * (x + i) + owner) * BLOCK, BLOCK)
                    bands[a, :, pl.ds(start, BLOCK)] = value
        width = bands.shape[2]
        copies.append(pltpu.make_async_copy(bands.at[a], out.at[0, :, a * width:(a + 1) * width], done.at[a]))
        copies[a].start()
    s = jnp.where(core == parity, mine[chip, block], theirs[chip, block])
    right[...] = jnp.dot(inverse[...], s, precision=HIGHEST, preferred_element_type=jnp.float32)
    for copy in copies:
        copy.wait()


def update_far(place, weights, inverse, mine, theirs, near, gradient, error):
    _, rows, cols = gradient.shape
    chips, groups, rank, _ = mine.shape
    return pl.pallas_call(
        far_kernel,
        in_specs=[SCALARS] + [VECTORS] * 7,
        out_specs=[pl.BlockSpec(memory_space=pl.ANY), VECTORS],
        out_shape=[jax.ShapeDtypeStruct(gradient.shape, gradient.dtype),
                   jax.ShapeDtypeStruct((rank, BLOCK), jnp.float32)],
        scratch_shapes=[pltpu.VMEM((groups, rows, cols // groups), gradient.dtype),
                        pltpu.SemaphoreType.DMA((groups,))],
        cost_estimate=pl.CostEstimate(
            flops=4 * rows * cols * rank, bytes_accessed=6 * rows * cols, transcendentals=0),
        compiler_params=PARAMS,
        name="update_far",
    )(place, weights, inverse, mine, theirs, near, gradient, error)


def body(gradient, error, q_prev):
    replicas = lax.axis_size("replica")
    shards = lax.axis_size("mp")
    rows, cols = gradient.shape[1:]
    rank = q_prev.shape[1]
    own = cols // replicas
    groups = own // BLOCK
    replica = lax.axis_index("replica").astype(jnp.int32)
    shard = lax.axis_index("mp").astype(jnp.int32)
    core = replica % CORES
    outer, inner = shard // replicas, shard % replicas
    chip_groups = [[c + CORES * x for x in range(replicas // CORES)] for c in range(CORES)]

    keep, give = split_moment(core.reshape(1), gradient, error, own)
    paired, q_block = lax.optimization_barrier((keep + swap_cores(give, replicas), q_prev.T))
    parts = exchange(paired, "replica", chip_groups)

    def along(apart):
        return [(r * shards + o * replicas + i, i * shards + (o ^ apart) * replicas + r)
                for r in range(replicas) for o in range(groups) for i in range(replicas)]
    blocks = [lax.ppermute(q_block, ("replica", "mp"), along(apart)) for apart in range(groups)]
    mean, copies = product(outer.reshape(1), parts, blocks, replicas)

    p_mean, tiles = pack(exchange(copies, "replica"), mean, shards)
    packed = (shards, PACK, 1, BLOCK)
    tiles = exchange(tiles.reshape(packed), "mp").reshape(tiles.shape)
    tiles = exchange(total(tiles).reshape(packed), "mp").reshape(tiles.shape)
    copies, gram = unpack(tiles, replicas // CORES, groups, rank)
    mine = exchange(copies, "replica", chip_groups)

    lower = jnp.linalg.cholesky(gram)
    inverse = lax.linalg.triangular_solve(
        lower, jnp.eye(rank, dtype=jnp.float32), left_side=True, lower=True
    )
    p_factor, weights = factors(p_mean, inverse)
    mine, weights, inverse = lax.optimization_barrier((mine, weights, inverse))
    theirs = swap_cores(mine, replicas)

    place = jnp.stack([core, outer, inner // CORES, inner % CORES])
    near = update_near(place, weights, mine, gradient, error)
    new_error, right = update_far(place, weights, inverse, mine, theirs, near, gradient, error)
    return (new_error, right.T, p_factor)


def solution(mesh):
    return jax.shard_map(
        body,
        mesh=mesh,
        in_specs=(P("replica", "mp", None), P("replica", "mp", None), P("mp", None)),
        out_specs=(P("replica", "mp", None), P("mp", None), P("mp", None)),
        check_vma=False,
    )
```

```python
import jax
import jax.numpy as jnp
from jax import lax
from jax.experimental import pallas as pl
from jax.experimental.pallas import tpu as pltpu
from jax.sharding import PartitionSpec as P

HIGHEST = lax.Precision.HIGHEST
BLOCK = 128
CORES = 2
TILE = 8
PACK = 9
PARAMS = pltpu.CompilerParams(vmem_limit_bytes=16 * 2**20)


def exchange(value, axis, groups=None):
    return lax.all_to_all(value, axis, 0, 0, axis_index_groups=groups)


def swap_cores(value, replicas):
    return lax.ppermute(value, "replica", [(r, r ^ 1) for r in range(replicas)])


SCALARS = pl.BlockSpec(memory_space=pltpu.SMEM)
VECTORS = pl.BlockSpec(memory_space=pltpu.VMEM)


def moment_block(gradient, error, block):
    columns = pl.ds(pl.multiple_of(block * BLOCK, BLOCK), BLOCK)
    return gradient[0, :, columns].astype(jnp.float32) + error[0, :, columns].astype(jnp.float32)


def split_kernel(place, gradient, error, keep, give):
    chips, _, own = keep.shape
    for apart in range(chips):
        chip = place[1] ^ apart
        for out, core in ((keep, place[0]), (give, 1 - place[0])):
            for k in range(own // BLOCK):
                out[apart, :, k * BLOCK:(k + 1) * BLOCK] = moment_block(
                    gradient, error, CORES * (k * chips + chip) + core)


def split_moment(place, gradient, error, own):
    _, rows, cols = gradient.shape
    shape = jax.ShapeDtypeStruct((cols // own // CORES, rows, own), jnp.float32)
    return pl.pallas_call(
        split_kernel,
        in_specs=[SCALARS, VECTORS, VECTORS],
        out_shape=[shape, shape],
        cost_estimate=pl.CostEstimate(flops=rows * cols, bytes_accessed=8 * rows * cols, transcendentals=0),
        compiler_params=PARAMS,
        name="split_moment",
    )(place, gradient, error)


def product_kernel(own, one, two, three, q_blocks, mean, copies):
    mean[...] = (own[...] + one[...] + two[...] + three[...]) * (1.0 / copies.shape[0])
    q_own = jnp.concatenate([q_blocks[a] for a in range(q_blocks.shape[0])], axis=1)
    p = lax.dot_general(mean[...], q_own, (((1,), (1,)), ((), ())), precision=HIGHEST,
                        preferred_element_type=jnp.float32)
    half = p.shape[0] // 2
    folded = jnp.concatenate([p[:half], p[half:]], axis=1)
    for r in range(copies.shape[0]):
        copies[r] = folded


def product(parts, q_blocks, replicas):
    rows, own = parts[0].shape
    rank = q_blocks.shape[1]
    return pl.pallas_call(
        product_kernel,
        out_shape=[jax.ShapeDtypeStruct((rows, own), jnp.float32),
                   jax.ShapeDtypeStruct((replicas, rows // 2, 2 * rank), jnp.float32)],
        cost_estimate=pl.CostEstimate(
            flops=2 * rows * own * rank, bytes_accessed=4 * len(parts) * rows * own, transcendentals=0),
        compiler_params=PARAMS,
        name="product",
    )(*parts, q_blocks)


def pack_kernel(p_parts, mean, p_mean, tiles):
    folded = p_parts[0]
    for r in range(1, p_parts.shape[0]):
        folded = folded + p_parts[r]
    rank = folded.shape[1] // 2
    p = jnp.concatenate([folded[:, :rank], folded[:, rank:]], axis=0)
    p_mean[...] = p
    over_rows = (((0,), (0,)), ((), ()))
    s = lax.dot_general(p, mean[...], over_rows, precision=HIGHEST, preferred_element_type=jnp.float32)
    gram = lax.dot_general(p, p, over_rows, precision=HIGHEST, preferred_element_type=jnp.float32)
    gram = jnp.concatenate([gram] * (BLOCK // rank), axis=1)
    slabs = rank // TILE
    for a in range(mean.shape[1] // BLOCK):
        for b in range(slabs):
            t = a * slabs + b
            tiles[t * PACK:t * PACK + TILE] = s[b * TILE:(b + 1) * TILE, a * BLOCK:(a + 1) * BLOCK]
            tiles[t * PACK + TILE:(t + 1) * PACK] = gram[t:t + 1]


def pack(p_parts, mean, shards):
    rows, own = mean.shape
    rank = p_parts.shape[2] // 2
    return pl.pallas_call(
        pack_kernel,
        out_shape=[jax.ShapeDtypeStruct((rows, rank), jnp.float32),
                   jax.ShapeDtypeStruct((shards * PACK, BLOCK), jnp.float32)],
        cost_estimate=pl.CostEstimate(flops=2 * rows * own * rank, bytes_accessed=8 * mean.size, transcendentals=0),
        compiler_params=PARAMS,
        name="pack",
    )(p_parts, mean)


def total_kernel(tiles, copies):
    shards = tiles.shape[0] // PACK
    parts = [tiles[t * PACK:(t + 1) * PACK] for t in range(shards)]
    while len(parts) > 1:
        parts = [parts[i] + parts[i + 1] for i in range(0, len(parts), 2)]
    for t in range(shards):
        copies[t * PACK:(t + 1) * PACK] = parts[0]


def total(tiles):
    return pl.pallas_call(
        total_kernel,
        out_shape=jax.ShapeDtypeStruct(tiles.shape, tiles.dtype),
        cost_estimate=pl.CostEstimate(flops=tiles.size, bytes_accessed=8 * tiles.size, transcendentals=0),
        compiler_params=PARAMS,
        name="total",
    )(tiles)


def unpack_kernel(tiles, copies, gram):
    count, groups, rank, _ = copies.shape
    slabs = rank // TILE
    for a in range(groups):
        for b in range(slabs):
            t = a * slabs + b
            tile = tiles[t * PACK:t * PACK + TILE]
            for x in range(count):
                copies[x, a, b * TILE:(b + 1) * TILE] = tile
            gram[t:t + 1] = tiles[t * PACK + TILE:(t + 1) * PACK, :rank]


def unpack(tiles, count, groups, rank):
    return pl.pallas_call(
        unpack_kernel,
        out_shape=[jax.ShapeDtypeStruct((count, groups, rank, BLOCK), jnp.float32),
                   jax.ShapeDtypeStruct((rank, rank), jnp.float32)],
        cost_estimate=pl.CostEstimate(flops=0, bytes_accessed=tiles.size * 20, transcendentals=0),
        compiler_params=PARAMS,
        name="unpack",
    )(tiles)


def factors_kernel(p_mean, inverse, p_factor, weights):
    p = lax.dot_general(p_mean[...], inverse[...], (((1,), (1,)), ((), ())), precision=HIGHEST,
                        preferred_element_type=jnp.float32)
    w = jnp.dot(p, inverse[...], precision=HIGHEST, preferred_element_type=jnp.float32)
    p_factor[...] = p
    weights[...] = jnp.concatenate([w, w], axis=1)


def factors(p_mean, inverse):
    rows, rank = p_mean.shape
    return pl.pallas_call(
        factors_kernel,
        out_shape=[jax.ShapeDtypeStruct((rows, rank), jnp.float32),
                   jax.ShapeDtypeStruct((rows, 2 * rank), jnp.float32)],
        cost_estimate=pl.CostEstimate(flops=4 * rows * rank * rank, bytes_accessed=20 * rows * rank, transcendentals=0),
        compiler_params=PARAMS,
        name="factors",
    )(p_mean, inverse)


def halves(value, axis):
    high = value.astype(jnp.bfloat16)
    low = (value - high.astype(jnp.float32)).astype(jnp.bfloat16)
    return jnp.concatenate([high, low], axis=axis)


def remainder(factor, s, x, a, core, gradient, error):
    chips, _, rank, _ = s.shape
    stack = halves(jnp.concatenate([s[x, a], s[x + 1, a]], axis=1), 0)
    change = jnp.dot(factor, stack, preferred_element_type=jnp.float32)
    rows = change.shape[0] // 2
    change = change[:rows] + change[rows:]
    return [
        (moment_block(gradient, error, CORES * (a * chips + x + i) + core)
         - change[:, i * BLOCK:(i + 1) * BLOCK]).astype(gradient.dtype)
        for i in range(2)]


def near_kernel(place, weights, mine, gradient, error, out):
    chips, groups, _, _ = mine.shape
    factor = halves(weights[...], 0)
    for a in range(groups):
        for x in range(0, chips, 2):
            out[x, a], out[x + 1, a] = remainder(factor, mine, x, a, place[0], gradient, error)


def update_near(place, weights, mine, gradient, error):
    _, rows, cols = gradient.shape
    chips, groups, rank, _ = mine.shape
    return pl.pallas_call(
        near_kernel,
        in_specs=[SCALARS] + [VECTORS] * 4,
        out_shape=jax.ShapeDtypeStruct((chips, groups, rows, BLOCK), gradient.dtype),
        cost_estimate=pl.CostEstimate(
            flops=4 * rows * cols * rank, bytes_accessed=4 * rows * cols, transcendentals=0),
        compiler_params=PARAMS,
        name="update_near",
    )(place, weights, mine, gradient, error)


def far_kernel(place, weights, inverse, mine, theirs, near, gradient, error, out, right, bands, done):
    chips, groups, _, _ = mine.shape
    core, block, chip, parity = (place[i] for i in range(4))
    factor = halves(weights[...], 0)
    copies = []
    for a in range(groups):
        for x in range(0, chips, 2):
            far = remainder(factor, theirs, x, a, 1 - core, gradient, error)
            for i in range(2):
                for value, owner in ((near[x + i, a], core), (far[i], 1 - core)):
                    start = pl.multiple_of((CORES * (x + i) + owner) * BLOCK, BLOCK)
                    bands[a, :, pl.ds(start, BLOCK)] = value
        width = bands.shape[2]
        copies.append(pltpu.make_async_copy(bands.at[a], out.at[0, :, a * width:(a + 1) * width], done.at[a]))
        copies[a].start()
    s = jnp.where(core == parity, mine[chip, block], theirs[chip, block])
    right[...] = jnp.dot(inverse[...], s, precision=HIGHEST, preferred_element_type=jnp.float32)
    for copy in copies:
        copy.wait()


def update_far(place, weights, inverse, mine, theirs, near, gradient, error):
    _, rows, cols = gradient.shape
    chips, groups, rank, _ = mine.shape
    return pl.pallas_call(
        far_kernel,
        in_specs=[SCALARS] + [VECTORS] * 7,
        out_specs=[pl.BlockSpec(memory_space=pl.ANY), VECTORS],
        out_shape=[jax.ShapeDtypeStruct(gradient.shape, gradient.dtype),
                   jax.ShapeDtypeStruct((rank, BLOCK), jnp.float32)],
        scratch_shapes=[pltpu.VMEM((groups, rows, cols // groups), gradient.dtype),
                        pltpu.SemaphoreType.DMA((groups,))],
        cost_estimate=pl.CostEstimate(
            flops=4 * rows * cols * rank, bytes_accessed=6 * rows * cols, transcendentals=0),
        compiler_params=PARAMS,
        name="update_far",
    )(place, weights, inverse, mine, theirs, near, gradient, error)


def body(gradient, error, q_prev):
    replicas = lax.axis_size("replica")
    shards = lax.axis_size("mp")
    rows, cols = gradient.shape[1:]
    rank = q_prev.shape[1]
    own = cols // replicas
    groups = own // BLOCK
    replica = lax.axis_index("replica").astype(jnp.int32)
    shard = lax.axis_index("mp").astype(jnp.int32)
    core = replica % CORES
    outer, inner = shard // replicas, shard % replicas
    outer_groups = [[o * replicas + i for o in range(groups)] for i in range(replicas)]
    chip_groups = [[c + CORES * x for x in range(replicas // CORES)] for c in range(CORES)]

    q_block = lax.ppermute(q_prev.T, ("replica", "mp"), [
        (r * shards + o * replicas + i, i * shards + o * replicas + r)
        for r in range(replicas) for o in range(groups) for i in range(replicas)
    ])

    keep, give = split_moment(jnp.stack([core, replica // CORES]), gradient, error, own)
    came = swap_cores(give, replicas)
    paired = [keep[apart] + came[apart] for apart in range(replicas // CORES)]
    *paired, q_block = lax.optimization_barrier((*paired, q_block))
    parts = paired[:1] + [
        lax.ppermute(paired[apart], "replica", [(r, r ^ (CORES * apart)) for r in range(replicas)])
        for apart in range(1, len(paired))]
    q_copies = jnp.broadcast_to(q_block[None], (groups,) + q_block.shape)
    q_blocks = exchange(q_copies, "mp", outer_groups)
    mean, copies = product(parts, q_blocks, replicas)

    p_mean, tiles = pack(exchange(copies, "replica"), mean, shards)
    packed = (shards, PACK, 1, BLOCK)
    tiles = exchange(tiles.reshape(packed), "mp").reshape(tiles.shape)
    tiles = exchange(total(tiles).reshape(packed), "mp").reshape(tiles.shape)
    copies, gram = unpack(tiles, replicas // CORES, groups, rank)
    mine = exchange(copies, "replica", chip_groups)

    lower = jnp.linalg.cholesky(gram)
    inverse = lax.linalg.triangular_solve(
        lower, jnp.eye(rank, dtype=jnp.float32), left_side=True, lower=True
    )
    p_factor, weights = factors(p_mean, inverse)
    mine, weights, inverse = lax.optimization_barrier((mine, weights, inverse))
    theirs = swap_cores(mine, replicas)

    place = jnp.stack([core, outer, inner // CORES, inner % CORES])
    near = update_near(place, weights, mine, gradient, error)
    new_error, right = update_far(place, weights, inverse, mine, theirs, near, gradient, error)
    return (new_error, right.T, p_factor)


def solution(mesh):
    return jax.shard_map(
        body,
        mesh=mesh,
        in_specs=(P("replica", "mp", None), P("replica", "mp", None), P("mp", None)),
        out_specs=(P("replica", "mp", None), P("mp", None), P("mp", None)),
        check_vma=False,
    )
```

```python
import jax
import jax.numpy as jnp
from jax import lax
from jax.experimental import pallas as pl
from jax.experimental.pallas import tpu as pltpu
from jax.sharding import PartitionSpec as P

HIGHEST = lax.Precision.HIGHEST
BLOCK = 128
CORES = 2
TILE = 8
PACK = 9
PARAMS = pltpu.CompilerParams(vmem_limit_bytes=16 * 2**20)


def exchange(value, axis, groups=None):
    return lax.all_to_all(value, axis, 0, 0, axis_index_groups=groups)


def swap_cores(value, replicas):
    return lax.ppermute(value, "replica", [(r, r ^ 1) for r in range(replicas)])


SCALARS = pl.BlockSpec(memory_space=pltpu.SMEM)
VECTORS = pl.BlockSpec(memory_space=pltpu.VMEM)


def moment_block(gradient, error, block):
    columns = pl.ds(pl.multiple_of(block * BLOCK, BLOCK), BLOCK)
    return gradient[0, :, columns].astype(jnp.float32) + error[0, :, columns].astype(jnp.float32)


def split_kernel(core_ref, gradient, error, keep, give):
    chips, _, own = keep.shape
    for x in range(chips):
        for out, core in ((keep, core_ref[0]), (give, 1 - core_ref[0])):
            for k in range(own // BLOCK):
                out[x, :, k * BLOCK:(k + 1) * BLOCK] = moment_block(
                    gradient, error, CORES * (k * chips + x) + core)


def split_moment(core, gradient, error, own):
    _, rows, cols = gradient.shape
    shape = jax.ShapeDtypeStruct((cols // own // CORES, rows, own), jnp.float32)
    return pl.pallas_call(
        split_kernel,
        in_specs=[SCALARS, VECTORS, VECTORS],
        out_shape=[shape, shape],
        cost_estimate=pl.CostEstimate(flops=rows * cols, bytes_accessed=8 * rows * cols, transcendentals=0),
        compiler_params=PARAMS,
        name="split_moment",
    )(core, gradient, error)


def product_kernel(outer_ref, parts, *refs):
    *pairs, mean, copies, q_list = refs
    mean[...] = (parts[0] + parts[1] + parts[2] + parts[3]) * (1.0 / copies.shape[0])
    for i, pair in enumerate(pairs):
        q_list[2 * i:2 * (i + 1)] = pair[...]
    blocks = []
    for a in range(q_list.shape[0]):
        apart = outer_ref[0] ^ a
        blocks.append(q_list[((apart & 3) << 1) | (apart >> 2)])
    q_own = jnp.concatenate(blocks, axis=1)
    p = lax.dot_general(mean[...], q_own, (((1,), (1,)), ((), ())), precision=HIGHEST,
                        preferred_element_type=jnp.float32)
    half = p.shape[0] // 2
    folded = jnp.concatenate([p[:half], p[half:]], axis=1)
    for r in range(copies.shape[0]):
        copies[r] = folded


def product(outer, parts, pairs, replicas):
    _, rows, own = parts.shape
    rank = pairs[0].shape[1]
    return pl.pallas_call(
        product_kernel,
        in_specs=[SCALARS, VECTORS] + [VECTORS] * len(pairs),
        out_shape=[jax.ShapeDtypeStruct((rows, own), jnp.float32),
                   jax.ShapeDtypeStruct((replicas, rows // 2, 2 * rank), jnp.float32)],
        scratch_shapes=[pltpu.VMEM((2 * len(pairs), rank, BLOCK), jnp.float32)],
        cost_estimate=pl.CostEstimate(flops=2 * rows * own * rank, bytes_accessed=4 * parts.size, transcendentals=0),
        compiler_params=PARAMS,
        name="product",
    )(outer, parts, *pairs)


def pack_kernel(p_parts, mean, p_mean, tiles):
    folded = p_parts[0]
    for r in range(1, p_parts.shape[0]):
        folded = folded + p_parts[r]
    rank = folded.shape[1] // 2
    p = jnp.concatenate([folded[:, :rank], folded[:, rank:]], axis=0)
    p_mean[...] = p
    over_rows = (((0,), (0,)), ((), ()))
    s = lax.dot_general(p, mean[...], over_rows, precision=HIGHEST, preferred_element_type=jnp.float32)
    gram = lax.dot_general(p, p, over_rows, precision=HIGHEST, preferred_element_type=jnp.float32)
    gram = jnp.concatenate([gram] * (BLOCK // rank), axis=1)
    slabs = rank // TILE
    for a in range(mean.shape[1] // BLOCK):
        for b in range(slabs):
            t = a * slabs + b
            tiles[t * PACK:t * PACK + TILE] = s[b * TILE:(b + 1) * TILE, a * BLOCK:(a + 1) * BLOCK]
            tiles[t * PACK + TILE:(t + 1) * PACK] = gram[t:t + 1]


def pack(p_parts, mean, shards):
    rows, own = mean.shape
    rank = p_parts.shape[2] // 2
    return pl.pallas_call(
        pack_kernel,
        out_shape=[jax.ShapeDtypeStruct((rows, rank), jnp.float32),
                   jax.ShapeDtypeStruct((shards * PACK, BLOCK), jnp.float32)],
        cost_estimate=pl.CostEstimate(flops=2 * rows * own * rank, bytes_accessed=8 * mean.size, transcendentals=0),
        compiler_params=PARAMS,
        name="pack",
    )(p_parts, mean)


def total_kernel(tiles, copies):
    shards = tiles.shape[0] // PACK
    parts = [tiles[t * PACK:(t + 1) * PACK] for t in range(shards)]
    while len(parts) > 1:
        parts = [parts[i] + parts[i + 1] for i in range(0, len(parts), 2)]
    for t in range(shards):
        copies[t * PACK:(t + 1) * PACK] = parts[0]


def total(tiles):
    return pl.pallas_call(
        total_kernel,
        out_shape=jax.ShapeDtypeStruct(tiles.shape, tiles.dtype),
        cost_estimate=pl.CostEstimate(flops=tiles.size, bytes_accessed=8 * tiles.size, transcendentals=0),
        compiler_params=PARAMS,
        name="total",
    )(tiles)


def unpack_kernel(tiles, copies, gram):
    count, groups, rank, _ = copies.shape
    slabs = rank // TILE
    for a in range(groups):
        for b in range(slabs):
            t = a * slabs + b
            tile = tiles[t * PACK:t * PACK + TILE]
            for x in range(count):
                copies[x, a, b * TILE:(b + 1) * TILE] = tile
            gram[t:t + 1] = tiles[t * PACK + TILE:(t + 1) * PACK, :rank]


def unpack(tiles, count, groups, rank):
    return pl.pallas_call(
        unpack_kernel,
        out_shape=[jax.ShapeDtypeStruct((count, groups, rank, BLOCK), jnp.float32),
                   jax.ShapeDtypeStruct((rank, rank), jnp.float32)],
        cost_estimate=pl.CostEstimate(flops=0, bytes_accessed=tiles.size * 20, transcendentals=0),
        compiler_params=PARAMS,
        name="unpack",
    )(tiles)


def factors_kernel(p_mean, inverse, p_factor, weights):
    p = lax.dot_general(p_mean[...], inverse[...], (((1,), (1,)), ((), ())), precision=HIGHEST,
                        preferred_element_type=jnp.float32)
    w = jnp.dot(p, inverse[...], precision=HIGHEST, preferred_element_type=jnp.float32)
    p_factor[...] = p
    weights[...] = jnp.concatenate([w, w], axis=1)


def factors(p_mean, inverse):
    rows, rank = p_mean.shape
    return pl.pallas_call(
        factors_kernel,
        out_shape=[jax.ShapeDtypeStruct((rows, rank), jnp.float32),
                   jax.ShapeDtypeStruct((rows, 2 * rank), jnp.float32)],
        cost_estimate=pl.CostEstimate(flops=4 * rows * rank * rank, bytes_accessed=20 * rows * rank, transcendentals=0),
        compiler_params=PARAMS,
        name="factors",
    )(p_mean, inverse)


def halves(value, axis):
    high = value.astype(jnp.bfloat16)
    low = (value - high.astype(jnp.float32)).astype(jnp.bfloat16)
    return jnp.concatenate([high, low], axis=axis)


def remainder(factor, s, x, a, core, gradient, error):
    chips, _, rank, _ = s.shape
    stack = halves(jnp.concatenate([s[x, a], s[x + 1, a]], axis=1), 0)
    change = jnp.dot(factor, stack, preferred_element_type=jnp.float32)
    rows = change.shape[0] // 2
    change = change[:rows] + change[rows:]
    return [
        (moment_block(gradient, error, CORES * (a * chips + x + i) + core)
         - change[:, i * BLOCK:(i + 1) * BLOCK]).astype(gradient.dtype)
        for i in range(2)]


def near_kernel(place, weights, mine, gradient, error, out):
    chips, groups, _, _ = mine.shape
    factor = halves(weights[...], 0)
    for a in range(groups):
        for x in range(0, chips, 2):
            out[x, a], out[x + 1, a] = remainder(factor, mine, x, a, place[0], gradient, error)


def update_near(place, weights, mine, gradient, error):
    _, rows, cols = gradient.shape
    chips, groups, rank, _ = mine.shape
    return pl.pallas_call(
        near_kernel,
        in_specs=[SCALARS] + [VECTORS] * 4,
        out_shape=jax.ShapeDtypeStruct((chips, groups, rows, BLOCK), gradient.dtype),
        cost_estimate=pl.CostEstimate(
            flops=4 * rows * cols * rank, bytes_accessed=4 * rows * cols, transcendentals=0),
        compiler_params=PARAMS,
        name="update_near",
    )(place, weights, mine, gradient, error)


def far_kernel(place, weights, inverse, mine, theirs, near, gradient, error, out, right, bands, done):
    chips, groups, _, _ = mine.shape
    core, block, chip, parity = (place[i] for i in range(4))
    factor = halves(weights[...], 0)
    copies = []
    for a in range(groups):
        for x in range(0, chips, 2):
            far = remainder(factor, theirs, x, a, 1 - core, gradient, error)
            for i in range(2):
                for value, owner in ((near[x + i, a], core), (far[i], 1 - core)):
                    start = pl.multiple_of((CORES * (x + i) + owner) * BLOCK, BLOCK)
                    bands[a, :, pl.ds(start, BLOCK)] = value
        width = bands.shape[2]
        copies.append(pltpu.make_async_copy(bands.at[a], out.at[0, :, a * width:(a + 1) * width], done.at[a]))
        copies[a].start()
    s = jnp.where(core == parity, mine[chip, block], theirs[chip, block])
    right[...] = jnp.dot(inverse[...], s, precision=HIGHEST, preferred_element_type=jnp.float32)
    for copy in copies:
        copy.wait()


def update_far(place, weights, inverse, mine, theirs, near, gradient, error):
    _, rows, cols = gradient.shape
    chips, groups, rank, _ = mine.shape
    return pl.pallas_call(
        far_kernel,
        in_specs=[SCALARS] + [VECTORS] * 7,
        out_specs=[pl.BlockSpec(memory_space=pl.ANY), VECTORS],
        out_shape=[jax.ShapeDtypeStruct(gradient.shape, gradient.dtype),
                   jax.ShapeDtypeStruct((rank, BLOCK), jnp.float32)],
        scratch_shapes=[pltpu.VMEM((groups, rows, cols // groups), gradient.dtype),
                        pltpu.SemaphoreType.DMA((groups,))],
        cost_estimate=pl.CostEstimate(
            flops=4 * rows * cols * rank, bytes_accessed=6 * rows * cols, transcendentals=0),
        compiler_params=PARAMS,
        name="update_far",
    )(place, weights, inverse, mine, theirs, near, gradient, error)


def body(gradient, error, q_prev):
    replicas = lax.axis_size("replica")
    shards = lax.axis_size("mp")
    rows, cols = gradient.shape[1:]
    rank = q_prev.shape[1]
    own = cols // replicas
    groups = own // BLOCK
    replica = lax.axis_index("replica").astype(jnp.int32)
    shard = lax.axis_index("mp").astype(jnp.int32)
    core = replica % CORES
    outer, inner = shard // replicas, shard % replicas
    chip_groups = [[c + CORES * x for x in range(replicas // CORES)] for c in range(CORES)]

    q_block = lax.ppermute(q_prev.T[None], ("replica", "mp"), [
        (r * shards + o * replicas + i, i * shards + o * replicas + r)
        for r in range(replicas) for o in range(groups) for i in range(replicas)
    ])

    keep, give = split_moment(core.reshape(1), gradient, error, own)
    paired, q_block = lax.optimization_barrier((keep + swap_cores(give, replicas), q_block))
    parts = exchange(paired, "replica", chip_groups)

    def along(value, apart):
        return lax.ppermute(value, "mp", [(j, j ^ (apart * replicas)) for j in range(shards)])
    pair = jnp.concatenate([q_block, along(q_block, 4)], axis=0)
    pairs = [pair] + [along(pair, apart) for apart in (1, 2, 3)]
    mean, copies = product(outer.reshape(1), parts, pairs, replicas)

    p_mean, tiles = pack(exchange(copies, "replica"), mean, shards)
    packed = (shards, PACK, 1, BLOCK)
    tiles = exchange(tiles.reshape(packed), "mp").reshape(tiles.shape)
    tiles = exchange(total(tiles).reshape(packed), "mp").reshape(tiles.shape)
    copies, gram = unpack(tiles, replicas // CORES, groups, rank)
    mine = exchange(copies, "replica", chip_groups)

    lower = jnp.linalg.cholesky(gram)
    inverse = lax.linalg.triangular_solve(
        lower, jnp.eye(rank, dtype=jnp.float32), left_side=True, lower=True
    )
    p_factor, weights = factors(p_mean, inverse)
    mine, weights, inverse = lax.optimization_barrier((mine, weights, inverse))
    theirs = swap_cores(mine, replicas)

    place = jnp.stack([core, outer, inner // CORES, inner % CORES])
    near = update_near(place, weights, mine, gradient, error)
    new_error, right = update_far(place, weights, inverse, mine, theirs, near, gradient, error)
    return (new_error, right.T, p_factor)


def solution(mesh):
    return jax.shard_map(
        body,
        mesh=mesh,
        in_specs=(P("replica", "mp", None), P("replica", "mp", None), P("mp", None)),
        out_specs=(P("replica", "mp", None), P("mp", None), P("mp", None)),
        check_vma=False,
    )
```

```python
import jax
import jax.numpy as jnp
from jax import lax
from jax.experimental import pallas as pl
from jax.experimental.pallas import tpu as pltpu
from jax.sharding import PartitionSpec as P

HIGHEST = lax.Precision.HIGHEST
BLOCK = 128
CORES = 2
TILE = 8
PACK = 9
PARAMS = pltpu.CompilerParams(vmem_limit_bytes=16 * 2**20)


def exchange(value, axis, groups=None):
    return lax.all_to_all(value, axis, 0, 0, axis_index_groups=groups)


def swap_cores(value, replicas):
    return lax.ppermute(value, "replica", [(r, r ^ 1) for r in range(replicas)])


SCALARS = pl.BlockSpec(memory_space=pltpu.SMEM)
VECTORS = pl.BlockSpec(memory_space=pltpu.VMEM)


def moment_block(gradient, error, block):
    columns = pl.ds(pl.multiple_of(block * BLOCK, BLOCK), BLOCK)
    return gradient[0, :, columns].astype(jnp.float32) + error[0, :, columns].astype(jnp.float32)


def split_kernel(core_ref, gradient, error, keep, give):
    chips, _, own = keep.shape
    for x in range(chips):
        for out, core in ((keep, core_ref[0]), (give, 1 - core_ref[0])):
            for k in range(own // BLOCK):
                out[x, :, k * BLOCK:(k + 1) * BLOCK] = moment_block(
                    gradient, error, CORES * (k * chips + x) + core)


def split_moment(core, gradient, error, own):
    _, rows, cols = gradient.shape
    shape = jax.ShapeDtypeStruct((cols // own // CORES, rows, own), jnp.float32)
    return pl.pallas_call(
        split_kernel,
        in_specs=[SCALARS, VECTORS, VECTORS],
        out_shape=[shape, shape],
        cost_estimate=pl.CostEstimate(flops=rows * cols, bytes_accessed=8 * rows * cols, transcendentals=0),
        compiler_params=PARAMS,
        name="split_moment",
    )(core, gradient, error)


def product_kernel(outer_ref, parts, *refs):
    *pairs, mean, copies, q_list = refs
    mean[...] = (parts[0] + parts[1] + parts[2] + parts[3]) * (1.0 / copies.shape[0])
    for i, pair in enumerate(pairs):
        q_list[2 * i:2 * (i + 1)] = pair[...]
    blocks = []
    for a in range(q_list.shape[0]):
        apart = outer_ref[0] ^ a
        blocks.append(q_list[((apart & 3) << 1) | (apart >> 2)])
    q_own = jnp.concatenate(blocks, axis=1)
    p = lax.dot_general(mean[...], q_own, (((1,), (1,)), ((), ())), precision=HIGHEST,
                        preferred_element_type=jnp.float32)
    half = p.shape[0] // 2
    folded = jnp.concatenate([p[:half], p[half:]], axis=1)
    for r in range(copies.shape[0]):
        copies[r] = folded


def product(outer, parts, pairs, replicas):
    _, rows, own = parts.shape
    rank = pairs[0].shape[1]
    return pl.pallas_call(
        product_kernel,
        in_specs=[SCALARS, VECTORS] + [VECTORS] * len(pairs),
        out_shape=[jax.ShapeDtypeStruct((rows, own), jnp.float32),
                   jax.ShapeDtypeStruct((replicas, rows // 2, 2 * rank), jnp.float32)],
        scratch_shapes=[pltpu.VMEM((2 * len(pairs), rank, BLOCK), jnp.float32)],
        cost_estimate=pl.CostEstimate(flops=2 * rows * own * rank, bytes_accessed=4 * parts.size, transcendentals=0),
        compiler_params=PARAMS,
        name="product",
    )(outer, parts, *pairs)


def pack_kernel(p_parts, mean, p_mean, tiles):
    folded = p_parts[0]
    for r in range(1, p_parts.shape[0]):
        folded = folded + p_parts[r]
    rank = folded.shape[1] // 2
    p = jnp.concatenate([folded[:, :rank], folded[:, rank:]], axis=0)
    p_mean[...] = p
    over_rows = (((0,), (0,)), ((), ()))
    s = lax.dot_general(p, mean[...], over_rows, precision=HIGHEST, preferred_element_type=jnp.float32)
    gram = lax.dot_general(p, p, over_rows, precision=HIGHEST, preferred_element_type=jnp.float32)
    gram = jnp.concatenate([gram] * (BLOCK // rank), axis=1)
    slabs = rank // TILE
    for a in range(mean.shape[1] // BLOCK):
        for b in range(slabs):
            t = a * slabs + b
            tiles[t * PACK:t * PACK + TILE] = s[b * TILE:(b + 1) * TILE, a * BLOCK:(a + 1) * BLOCK]
            tiles[t * PACK + TILE:(t + 1) * PACK] = gram[t:t + 1]


def pack(p_parts, mean, shards):
    rows, own = mean.shape
    rank = p_parts.shape[2] // 2
    return pl.pallas_call(
        pack_kernel,
        out_shape=[jax.ShapeDtypeStruct((rows, rank), jnp.float32),
                   jax.ShapeDtypeStruct((shards * PACK, BLOCK), jnp.float32)],
        cost_estimate=pl.CostEstimate(flops=2 * rows * own * rank, bytes_accessed=8 * mean.size, transcendentals=0),
        compiler_params=PARAMS,
        name="pack",
    )(p_parts, mean)


def total_kernel(tiles, copies):
    shards = tiles.shape[0] // PACK
    parts = [tiles[t * PACK:(t + 1) * PACK] for t in range(shards)]
    while len(parts) > 1:
        parts = [parts[i] + parts[i + 1] for i in range(0, len(parts), 2)]
    for t in range(shards):
        copies[t * PACK:(t + 1) * PACK] = parts[0]


def total(tiles):
    return pl.pallas_call(
        total_kernel,
        out_shape=jax.ShapeDtypeStruct(tiles.shape, tiles.dtype),
        cost_estimate=pl.CostEstimate(flops=tiles.size, bytes_accessed=8 * tiles.size, transcendentals=0),
        compiler_params=PARAMS,
        name="total",
    )(tiles)


def unpack_kernel(tiles, copies, gram):
    count, groups, rank, _ = copies.shape
    slabs = rank // TILE
    for a in range(groups):
        for b in range(slabs):
            t = a * slabs + b
            tile = tiles[t * PACK:t * PACK + TILE]
            for x in range(count):
                copies[x, a, b * TILE:(b + 1) * TILE] = tile
            gram[t:t + 1] = tiles[t * PACK + TILE:(t + 1) * PACK, :rank]


def unpack(tiles, count, groups, rank):
    return pl.pallas_call(
        unpack_kernel,
        out_shape=[jax.ShapeDtypeStruct((count, groups, rank, BLOCK), jnp.float32),
                   jax.ShapeDtypeStruct((rank, rank), jnp.float32)],
        cost_estimate=pl.CostEstimate(flops=0, bytes_accessed=tiles.size * 20, transcendentals=0),
        compiler_params=PARAMS,
        name="unpack",
    )(tiles)


def factors_kernel(p_mean, inverse, p_factor, weights):
    p = lax.dot_general(p_mean[...], inverse[...], (((1,), (1,)), ((), ())), precision=HIGHEST,
                        preferred_element_type=jnp.float32)
    w = jnp.dot(p, inverse[...], precision=HIGHEST, preferred_element_type=jnp.float32)
    p_factor[...] = p
    weights[...] = jnp.concatenate([w, w], axis=1)


def factors(p_mean, inverse):
    rows, rank = p_mean.shape
    return pl.pallas_call(
        factors_kernel,
        out_shape=[jax.ShapeDtypeStruct((rows, rank), jnp.float32),
                   jax.ShapeDtypeStruct((rows, 2 * rank), jnp.float32)],
        cost_estimate=pl.CostEstimate(flops=4 * rows * rank * rank, bytes_accessed=20 * rows * rank, transcendentals=0),
        compiler_params=PARAMS,
        name="factors",
    )(p_mean, inverse)


def halves(value, axis):
    high = value.astype(jnp.bfloat16)
    low = (value - high.astype(jnp.float32)).astype(jnp.bfloat16)
    return jnp.concatenate([high, low], axis=axis)


def remainder(factor, s, x, a, core, gradient, error):
    chips, _, rank, _ = s.shape
    stack = halves(jnp.concatenate([s[x, a], s[x + 1, a]], axis=1), 0)
    change = jnp.dot(factor, stack, preferred_element_type=jnp.float32)
    rows = change.shape[0] // 2
    change = change[:rows] + change[rows:]
    return [
        (moment_block(gradient, error, CORES * (a * chips + x + i) + core)
         - change[:, i * BLOCK:(i + 1) * BLOCK]).astype(gradient.dtype)
        for i in range(2)]


def near_kernel(place, weights, mine, gradient, error, out):
    chips, groups, _, _ = mine.shape
    factor = halves(weights[...], 0)
    for a in range(groups):
        for x in range(0, chips, 2):
            out[x, a], out[x + 1, a] = remainder(factor, mine, x, a, place[0], gradient, error)


def update_near(place, weights, mine, gradient, error):
    _, rows, cols = gradient.shape
    chips, groups, rank, _ = mine.shape
    return pl.pallas_call(
        near_kernel,
        in_specs=[SCALARS] + [VECTORS] * 4,
        out_shape=jax.ShapeDtypeStruct((chips, groups, rows, BLOCK), gradient.dtype),
        cost_estimate=pl.CostEstimate(
            flops=4 * rows * cols * rank, bytes_accessed=4 * rows * cols, transcendentals=0),
        compiler_params=PARAMS,
        name="update_near",
    )(place, weights, mine, gradient, error)


def far_kernel(place, weights, inverse, mine, theirs, near, gradient, error, out, right, bands, done):
    chips, groups, _, _ = mine.shape
    core, block, chip, parity = (place[i] for i in range(4))
    factor = halves(weights[...], 0)
    copies = []
    for a in range(groups):
        for x in range(0, chips, 2):
            far = remainder(factor, theirs, x, a, 1 - core, gradient, error)
            for i in range(2):
                for value, owner in ((near[x + i, a], core), (far[i], 1 - core)):
                    start = pl.multiple_of((CORES * (x + i) + owner) * BLOCK, BLOCK)
                    bands[a, :, pl.ds(start, BLOCK)] = value
        width = bands.shape[2]
        copies.append(pltpu.make_async_copy(bands.at[a], out.at[0, :, a * width:(a + 1) * width], done.at[a]))
        copies[a].start()
    s = jnp.where(core == parity, mine[chip, block], theirs[chip, block])
    right[...] = jnp.dot(inverse[...], s, precision=HIGHEST, preferred_element_type=jnp.float32)
    for copy in copies:
        copy.wait()


def update_far(place, weights, inverse, mine, theirs, near, gradient, error):
    _, rows, cols = gradient.shape
    chips, groups, rank, _ = mine.shape
    return pl.pallas_call(
        far_kernel,
        in_specs=[SCALARS] + [VECTORS] * 7,
        out_specs=[pl.BlockSpec(memory_space=pl.ANY), VECTORS],
        out_shape=[jax.ShapeDtypeStruct(gradient.shape, gradient.dtype),
                   jax.ShapeDtypeStruct((rank, BLOCK), jnp.float32)],
        scratch_shapes=[pltpu.VMEM((groups, rows, cols // groups), gradient.dtype),
                        pltpu.SemaphoreType.DMA((groups,))],
        cost_estimate=pl.CostEstimate(
            flops=4 * rows * cols * rank, bytes_accessed=6 * rows * cols, transcendentals=0),
        compiler_params=PARAMS,
        name="update_far",
    )(place, weights, inverse, mine, theirs, near, gradient, error)


def body(gradient, error, q_prev):
    replicas = lax.axis_size("replica")
    shards = lax.axis_size("mp")
    rows, cols = gradient.shape[1:]
    rank = q_prev.shape[1]
    own = cols // replicas
    groups = own // BLOCK
    replica = lax.axis_index("replica").astype(jnp.int32)
    shard = lax.axis_index("mp").astype(jnp.int32)
    core = replica % CORES
    outer, inner = shard // replicas, shard % replicas
    chip_groups = [[c + CORES * x for x in range(replicas // CORES)] for c in range(CORES)]

    q_block = lax.ppermute(q_prev.T[None], ("replica", "mp"), [
        (r * shards + o * replicas + i, i * shards + o * replicas + r)
        for r in range(replicas) for o in range(groups) for i in range(replicas)
    ])

    keep, give = split_moment(core.reshape(1), gradient, error, own)
    give, q_block = lax.optimization_barrier((give, q_block))

    def along(value, apart):
        return lax.ppermute(value, "mp", [(j, j ^ (apart * replicas)) for j in range(shards)])
    pair = jnp.concatenate([q_block, along(q_block, 4)], axis=0)
    paired, pair = lax.optimization_barrier((keep + swap_cores(give, replicas), pair))
    parts = exchange(paired, "replica", chip_groups)
    pairs = [pair] + [along(pair, apart) for apart in (1, 2, 3)]
    mean, copies = product(outer.reshape(1), parts, pairs, replicas)

    p_mean, tiles = pack(exchange(copies, "replica"), mean, shards)
    packed = (shards, PACK, 1, BLOCK)
    tiles = exchange(tiles.reshape(packed), "mp").reshape(tiles.shape)
    tiles = exchange(total(tiles).reshape(packed), "mp").reshape(tiles.shape)
    copies, gram = unpack(tiles, replicas // CORES, groups, rank)
    mine = exchange(copies, "replica", chip_groups)

    lower = jnp.linalg.cholesky(gram)
    inverse = lax.linalg.triangular_solve(
        lower, jnp.eye(rank, dtype=jnp.float32), left_side=True, lower=True
    )
    p_factor, weights = factors(p_mean, inverse)
    mine, weights, inverse = lax.optimization_barrier((mine, weights, inverse))
    theirs = swap_cores(mine, replicas)

    place = jnp.stack([core, outer, inner // CORES, inner % CORES])
    near = update_near(place, weights, mine, gradient, error)
    new_error, right = update_far(place, weights, inverse, mine, theirs, near, gradient, error)
    return (new_error, right.T, p_factor)


def solution(mesh):
    return jax.shard_map(
        body,
        mesh=mesh,
        in_specs=(P("replica", "mp", None), P("replica", "mp", None), P("mp", None)),
        out_specs=(P("replica", "mp", None), P("mp", None), P("mp", None)),
        check_vma=False,
    )
```

```python
import jax
import jax.numpy as jnp
from jax import lax
from jax.experimental import pallas as pl
from jax.experimental.pallas import tpu as pltpu
from jax.sharding import PartitionSpec as P

HIGHEST = lax.Precision.HIGHEST
BLOCK = 128
CORES = 2
TILE = 8
PACK = 9
PARAMS = pltpu.CompilerParams(vmem_limit_bytes=16 * 2**20)


def exchange(value, axis, groups=None):
    return lax.all_to_all(value, axis, 0, 0, axis_index_groups=groups)


def swap_cores(value, replicas):
    return lax.ppermute(value, "replica", [(r, r ^ 1) for r in range(replicas)])


SCALARS = pl.BlockSpec(memory_space=pltpu.SMEM)
VECTORS = pl.BlockSpec(memory_space=pltpu.VMEM)


def moment_block(gradient, error, block):
    columns = pl.ds(pl.multiple_of(block * BLOCK, BLOCK), BLOCK)
    return gradient[0, :, columns].astype(jnp.float32) + error[0, :, columns].astype(jnp.float32)


def split_kernel(core_ref, gradient, error, keep, give):
    chips, _, own = keep.shape
    for x in range(chips):
        for out, core in ((keep, core_ref[0]), (give, 1 - core_ref[0])):
            for k in range(own // BLOCK):
                out[x, :, k * BLOCK:(k + 1) * BLOCK] = moment_block(
                    gradient, error, CORES * (k * chips + x) + core)


def split_moment(core, gradient, error, own):
    _, rows, cols = gradient.shape
    shape = jax.ShapeDtypeStruct((cols // own // CORES, rows, own), jnp.float32)
    return pl.pallas_call(
        split_kernel,
        in_specs=[SCALARS, VECTORS, VECTORS],
        out_shape=[shape, shape],
        cost_estimate=pl.CostEstimate(flops=rows * cols, bytes_accessed=8 * rows * cols, transcendentals=0),
        compiler_params=PARAMS,
        name="split_moment",
    )(core, gradient, error)


def product_kernel(outer_ref, parts, *refs):
    *pairs, mean, copies, q_list = refs
    mean[...] = (parts[0] + parts[1] + parts[2] + parts[3]) * (1.0 / copies.shape[0])
    for i, pair in enumerate(pairs):
        q_list[2 * i:2 * (i + 1)] = pair[...]
    blocks = []
    for a in range(q_list.shape[0]):
        apart = outer_ref[0] ^ a
        blocks.append(q_list[apart])
    q_own = jnp.concatenate(blocks, axis=1)
    p = lax.dot_general(mean[...], q_own, (((1,), (1,)), ((), ())), precision=HIGHEST,
                        preferred_element_type=jnp.float32)
    half = p.shape[0] // 2
    folded = jnp.concatenate([p[:half], p[half:]], axis=1)
    for r in range(copies.shape[0]):
        copies[r] = folded


def product(outer, parts, pairs, replicas):
    _, rows, own = parts.shape
    rank = pairs[0].shape[1]
    return pl.pallas_call(
        product_kernel,
        in_specs=[SCALARS, VECTORS] + [VECTORS] * len(pairs),
        out_shape=[jax.ShapeDtypeStruct((rows, own), jnp.float32),
                   jax.ShapeDtypeStruct((replicas, rows // 2, 2 * rank), jnp.float32)],
        scratch_shapes=[pltpu.VMEM((2 * len(pairs), rank, BLOCK), jnp.float32)],
        cost_estimate=pl.CostEstimate(flops=2 * rows * own * rank, bytes_accessed=4 * parts.size, transcendentals=0),
        compiler_params=PARAMS,
        name="product",
    )(outer, parts, *pairs)


def pack_kernel(p_parts, mean, p_mean, tiles):
    folded = p_parts[0]
    for r in range(1, p_parts.shape[0]):
        folded = folded + p_parts[r]
    rank = folded.shape[1] // 2
    p = jnp.concatenate([folded[:, :rank], folded[:, rank:]], axis=0)
    p_mean[...] = p
    over_rows = (((0,), (0,)), ((), ()))
    s = lax.dot_general(p, mean[...], over_rows, precision=HIGHEST, preferred_element_type=jnp.float32)
    gram = lax.dot_general(p, p, over_rows, precision=HIGHEST, preferred_element_type=jnp.float32)
    gram = jnp.concatenate([gram] * (BLOCK // rank), axis=1)
    slabs = rank // TILE
    for a in range(mean.shape[1] // BLOCK):
        for b in range(slabs):
            t = a * slabs + b
            tiles[t * PACK:t * PACK + TILE] = s[b * TILE:(b + 1) * TILE, a * BLOCK:(a + 1) * BLOCK]
            tiles[t * PACK + TILE:(t + 1) * PACK] = gram[t:t + 1]


def pack(p_parts, mean, shards):
    rows, own = mean.shape
    rank = p_parts.shape[2] // 2
    return pl.pallas_call(
        pack_kernel,
        out_shape=[jax.ShapeDtypeStruct((rows, rank), jnp.float32),
                   jax.ShapeDtypeStruct((shards * PACK, BLOCK), jnp.float32)],
        cost_estimate=pl.CostEstimate(flops=2 * rows * own * rank, bytes_accessed=8 * mean.size, transcendentals=0),
        compiler_params=PARAMS,
        name="pack",
    )(p_parts, mean)


def total_kernel(tiles, copies):
    shards = tiles.shape[0] // PACK
    parts = [tiles[t * PACK:(t + 1) * PACK] for t in range(shards)]
    while len(parts) > 1:
        parts = [parts[i] + parts[i + 1] for i in range(0, len(parts), 2)]
    for t in range(shards):
        copies[t * PACK:(t + 1) * PACK] = parts[0]


def total(tiles):
    return pl.pallas_call(
        total_kernel,
        out_shape=jax.ShapeDtypeStruct(tiles.shape, tiles.dtype),
        cost_estimate=pl.CostEstimate(flops=tiles.size, bytes_accessed=8 * tiles.size, transcendentals=0),
        compiler_params=PARAMS,
        name="total",
    )(tiles)


def unpack_kernel(tiles, copies, gram):
    count, groups, rank, _ = copies.shape
    slabs = rank // TILE
    for a in range(groups):
        for b in range(slabs):
            t = a * slabs + b
            tile = tiles[t * PACK:t * PACK + TILE]
            for x in range(count):
                copies[x, a, b * TILE:(b + 1) * TILE] = tile
            gram[t:t + 1] = tiles[t * PACK + TILE:(t + 1) * PACK, :rank]


def unpack(tiles, count, groups, rank):
    return pl.pallas_call(
        unpack_kernel,
        out_shape=[jax.ShapeDtypeStruct((count, groups, rank, BLOCK), jnp.float32),
                   jax.ShapeDtypeStruct((rank, rank), jnp.float32)],
        cost_estimate=pl.CostEstimate(flops=0, bytes_accessed=tiles.size * 20, transcendentals=0),
        compiler_params=PARAMS,
        name="unpack",
    )(tiles)


def factors_kernel(p_mean, inverse, p_factor, weights):
    p = lax.dot_general(p_mean[...], inverse[...], (((1,), (1,)), ((), ())), precision=HIGHEST,
                        preferred_element_type=jnp.float32)
    w = jnp.dot(p, inverse[...], precision=HIGHEST, preferred_element_type=jnp.float32)
    p_factor[...] = p
    weights[...] = jnp.concatenate([w, w], axis=1)


def factors(p_mean, inverse):
    rows, rank = p_mean.shape
    return pl.pallas_call(
        factors_kernel,
        out_shape=[jax.ShapeDtypeStruct((rows, rank), jnp.float32),
                   jax.ShapeDtypeStruct((rows, 2 * rank), jnp.float32)],
        cost_estimate=pl.CostEstimate(flops=4 * rows * rank * rank, bytes_accessed=20 * rows * rank, transcendentals=0),
        compiler_params=PARAMS,
        name="factors",
    )(p_mean, inverse)


def halves(value, axis):
    high = value.astype(jnp.bfloat16)
    low = (value - high.astype(jnp.float32)).astype(jnp.bfloat16)
    return jnp.concatenate([high, low], axis=axis)


def remainder(factor, s, x, a, core, gradient, error):
    chips, _, rank, _ = s.shape
    stack = halves(jnp.concatenate([s[x, a], s[x + 1, a]], axis=1), 0)
    change = jnp.dot(factor, stack, preferred_element_type=jnp.float32)
    rows = change.shape[0] // 2
    change = change[:rows] + change[rows:]
    return [
        (moment_block(gradient, error, CORES * (a * chips + x + i) + core)
         - change[:, i * BLOCK:(i + 1) * BLOCK]).astype(gradient.dtype)
        for i in range(2)]


def half_kernel(factor, s, core, gradient, error, out, blocks, done):
    chips, groups, _, _ = s.shape
    copies = []
    for a in range(groups):
        for x in range(0, chips, 2):
            blocks[a, x], blocks[a, x + 1] = remainder(factor, s, x, a, core, gradient, error)
            for i in (x, x + 1):
                start = pl.multiple_of((CORES * (a * chips + i) + core) * BLOCK, BLOCK)
                copies.append(pltpu.make_async_copy(
                    blocks.at[a, i], out.at[0, :, pl.ds(start, BLOCK)], done.at[a, i]))
                copies[-1].start()
    return copies


def near_kernel(place, weights, mine, gradient, error, out, blocks, done):
    factor = halves(weights[...], 0)
    for copy in half_kernel(factor, mine, place[0], gradient, error, out, blocks, done):
        copy.wait()


def half_scratch(s, gradient):
    chips, groups, _, _ = s.shape
    return [pltpu.VMEM((groups, chips, gradient.shape[1], BLOCK), gradient.dtype),
            pltpu.SemaphoreType.DMA((groups, chips))]


def half_cost(s, gradient):
    _, rows, cols = gradient.shape
    return pl.CostEstimate(flops=4 * rows * cols * s.shape[2], bytes_accessed=4 * rows * cols, transcendentals=0)


def update_near(place, weights, mine, gradient, error):
    return pl.pallas_call(
        near_kernel,
        in_specs=[SCALARS] + [VECTORS] * 4,
        out_specs=pl.BlockSpec(memory_space=pl.ANY),
        out_shape=jax.ShapeDtypeStruct(gradient.shape, gradient.dtype),
        scratch_shapes=half_scratch(mine, gradient),
        cost_estimate=half_cost(mine, gradient),
        compiler_params=PARAMS,
        name="update_near",
    )(place, weights, mine, gradient, error)


def far_kernel(place, weights, inverse, mine, theirs, gradient, error, near, out, right, blocks, done):
    core, block, chip, parity = (place[i] for i in range(4))
    factor = halves(weights[...], 0)
    copies = half_kernel(factor, theirs, 1 - core, gradient, error, out, blocks, done)
    s = jnp.where(core == parity, mine[chip, block], theirs[chip, block])
    right[...] = jnp.dot(inverse[...], s, precision=HIGHEST, preferred_element_type=jnp.float32)
    for copy in copies:
        copy.wait()


def update_far(place, weights, inverse, mine, theirs, near, gradient, error):
    rank = mine.shape[2]
    return pl.pallas_call(
        far_kernel,
        in_specs=[SCALARS] + [VECTORS] * 6 + [pl.BlockSpec(memory_space=pl.ANY)],
        out_specs=[pl.BlockSpec(memory_space=pl.ANY), VECTORS],
        out_shape=[jax.ShapeDtypeStruct(gradient.shape, gradient.dtype),
                   jax.ShapeDtypeStruct((rank, BLOCK), jnp.float32)],
        input_output_aliases={7: 0},
        scratch_shapes=half_scratch(theirs, gradient),
        cost_estimate=half_cost(theirs, gradient),
        compiler_params=PARAMS,
        name="update_far",
    )(place, weights, inverse, mine, theirs, gradient, error, near)


def body(gradient, error, q_prev):
    replicas = lax.axis_size("replica")
    shards = lax.axis_size("mp")
    rows, cols = gradient.shape[1:]
    rank = q_prev.shape[1]
    own = cols // replicas
    groups = own // BLOCK
    replica = lax.axis_index("replica").astype(jnp.int32)
    shard = lax.axis_index("mp").astype(jnp.int32)
    core = replica % CORES
    outer, inner = shard // replicas, shard % replicas
    chip_groups = [[c + CORES * x for x in range(replicas // CORES)] for c in range(CORES)]

    q_block = lax.ppermute(q_prev.T[None], ("replica", "mp"), [
        (r * shards + o * replicas + i, i * shards + o * replicas + r)
        for r in range(replicas) for o in range(groups) for i in range(replicas)
    ])

    keep, give = split_moment(core.reshape(1), gradient, error, own)
    give, q_block = lax.optimization_barrier((give, q_block))

    def along(value, apart):
        return lax.ppermute(value, "mp", [(j, j ^ (apart * replicas)) for j in range(shards)])
    pair = jnp.concatenate([q_block, along(q_block, 1)], axis=0)
    paired, pair = lax.optimization_barrier((keep + swap_cores(give, replicas), pair))
    parts = exchange(paired, "replica", chip_groups)
    pairs = [pair] + [along(pair, apart) for apart in (2, 4, 6)]
    mean, copies = product(outer.reshape(1), parts, pairs, replicas)

    p_mean, tiles = pack(exchange(copies, "replica"), mean, shards)
    packed = (shards, PACK, 1, BLOCK)
    tiles = exchange(tiles.reshape(packed), "mp").reshape(tiles.shape)
    tiles = exchange(total(tiles).reshape(packed), "mp").reshape(tiles.shape)
    copies, gram = unpack(tiles, replicas // CORES, groups, rank)
    mine = exchange(copies, "replica", chip_groups)

    lower = jnp.linalg.cholesky(gram)
    inverse = lax.linalg.triangular_solve(
        lower, jnp.eye(rank, dtype=jnp.float32), left_side=True, lower=True
    )
    p_factor, weights = factors(p_mean, inverse)
    mine, weights, inverse = lax.optimization_barrier((mine, weights, inverse))
    theirs = swap_cores(mine, replicas)

    place = jnp.stack([core, outer, inner // CORES, inner % CORES])
    near = update_near(place, weights, mine, gradient, error)
    new_error, right = update_far(place, weights, inverse, mine, theirs, near, gradient, error)
    return (new_error, right.T, p_factor)


def solution(mesh):
    return jax.shard_map(
        body,
        mesh=mesh,
        in_specs=(P("replica", "mp", None), P("replica", "mp", None), P("mp", None)),
        out_specs=(P("replica", "mp", None), P("mp", None), P("mp", None)),
        check_vma=False,
    )
```

```python
import jax
import jax.numpy as jnp
from jax import lax
from jax.experimental import pallas as pl
from jax.experimental.pallas import tpu as pltpu
from jax.sharding import PartitionSpec as P

HIGHEST = lax.Precision.HIGHEST
BLOCK = 128
CORES = 2
TILE = 8
PACK = 9
PARAMS = pltpu.CompilerParams(vmem_limit_bytes=16 * 2**20)


def exchange(value, axis, groups=None):
    return lax.all_to_all(value, axis, 0, 0, axis_index_groups=groups)


def swap_cores(value, replicas):
    return lax.ppermute(value, "replica", [(r, r ^ 1) for r in range(replicas)])


SCALARS = pl.BlockSpec(memory_space=pltpu.SMEM)
VECTORS = pl.BlockSpec(memory_space=pltpu.VMEM)


def moment_block(gradient, error, block):
    columns = pl.ds(pl.multiple_of(block * BLOCK, BLOCK), BLOCK)
    return gradient[0, :, columns].astype(jnp.float32) + error[0, :, columns].astype(jnp.float32)


def split_kernel(core_ref, gradient, error, keep, give):
    chips, _, own = keep.shape
    for x in range(chips):
        for out, core in ((keep, core_ref[0]), (give, 1 - core_ref[0])):
            for k in range(own // BLOCK):
                out[x, :, k * BLOCK:(k + 1) * BLOCK] = moment_block(
                    gradient, error, CORES * (k * chips + x) + core)


def split_moment(core, gradient, error, own):
    _, rows, cols = gradient.shape
    shape = jax.ShapeDtypeStruct((cols // own // CORES, rows, own), jnp.float32)
    return pl.pallas_call(
        split_kernel,
        in_specs=[SCALARS, VECTORS, VECTORS],
        out_shape=[shape, shape],
        cost_estimate=pl.CostEstimate(flops=rows * cols, bytes_accessed=8 * rows * cols, transcendentals=0),
        compiler_params=PARAMS,
        name="split_moment",
    )(core, gradient, error)


def product_kernel(outer_ref, parts, *refs):
    *pairs, mean, copies, q_list = refs
    mean[...] = (parts[0] + parts[1] + parts[2] + parts[3]) * (1.0 / copies.shape[0])
    for i, pair in enumerate(pairs):
        q_list[2 * i:2 * (i + 1)] = pair[...]
    blocks = []
    for a in range(q_list.shape[0]):
        apart = outer_ref[0] ^ a
        blocks.append(q_list[apart])
    q_own = jnp.concatenate(blocks, axis=1)
    p = lax.dot_general(mean[...], q_own, (((1,), (1,)), ((), ())), precision=HIGHEST,
                        preferred_element_type=jnp.float32)
    half = p.shape[0] // 2
    folded = jnp.concatenate([p[:half], p[half:]], axis=1)
    for r in range(copies.shape[0]):
        copies[r] = folded


def product(outer, parts, pairs, replicas):
    _, rows, own = parts.shape
    rank = pairs[0].shape[1]
    return pl.pallas_call(
        product_kernel,
        in_specs=[SCALARS, VECTORS] + [VECTORS] * len(pairs),
        out_shape=[jax.ShapeDtypeStruct((rows, own), jnp.float32),
                   jax.ShapeDtypeStruct((replicas, rows // 2, 2 * rank), jnp.float32)],
        scratch_shapes=[pltpu.VMEM((2 * len(pairs), rank, BLOCK), jnp.float32)],
        cost_estimate=pl.CostEstimate(flops=2 * rows * own * rank, bytes_accessed=4 * parts.size, transcendentals=0),
        compiler_params=PARAMS,
        name="product",
    )(outer, parts, *pairs)


def pack_kernel(p_parts, mean, p_mean, tiles):
    folded = p_parts[0]
    for r in range(1, p_parts.shape[0]):
        folded = folded + p_parts[r]
    rank = folded.shape[1] // 2
    p = jnp.concatenate([folded[:, :rank], folded[:, rank:]], axis=0)
    p_mean[...] = p
    over_rows = (((0,), (0,)), ((), ()))
    s = lax.dot_general(p, mean[...], over_rows, precision=HIGHEST, preferred_element_type=jnp.float32)
    gram = lax.dot_general(p, p, over_rows, precision=HIGHEST, preferred_element_type=jnp.float32)
    gram = jnp.concatenate([gram] * (BLOCK // rank), axis=1)
    slabs = rank // TILE
    for a in range(mean.shape[1] // BLOCK):
        for b in range(slabs):
            t = a * slabs + b
            tiles[t * PACK:t * PACK + TILE] = s[b * TILE:(b + 1) * TILE, a * BLOCK:(a + 1) * BLOCK]
            tiles[t * PACK + TILE:(t + 1) * PACK] = gram[t:t + 1]


def pack(p_parts, mean, shards):
    rows, own = mean.shape
    rank = p_parts.shape[2] // 2
    return pl.pallas_call(
        pack_kernel,
        out_shape=[jax.ShapeDtypeStruct((rows, rank), jnp.float32),
                   jax.ShapeDtypeStruct((shards * PACK, BLOCK), jnp.float32)],
        cost_estimate=pl.CostEstimate(flops=2 * rows * own * rank, bytes_accessed=8 * mean.size, transcendentals=0),
        compiler_params=PARAMS,
        name="pack",
    )(p_parts, mean)


def total_kernel(tiles, copies):
    shards = tiles.shape[0] // PACK
    parts = [tiles[t * PACK:(t + 1) * PACK] for t in range(shards)]
    while len(parts) > 1:
        parts = [parts[i] + parts[i + 1] for i in range(0, len(parts), 2)]
    for t in range(shards):
        copies[t * PACK:(t + 1) * PACK] = parts[0]


def total(tiles):
    return pl.pallas_call(
        total_kernel,
        out_shape=jax.ShapeDtypeStruct(tiles.shape, tiles.dtype),
        cost_estimate=pl.CostEstimate(flops=tiles.size, bytes_accessed=8 * tiles.size, transcendentals=0),
        compiler_params=PARAMS,
        name="total",
    )(tiles)


def unpack_kernel(tiles, copies, gram):
    count, groups, rank, _ = copies.shape
    slabs = rank // TILE
    for a in range(groups):
        for b in range(slabs):
            t = a * slabs + b
            tile = tiles[t * PACK:t * PACK + TILE]
            for x in range(count):
                copies[x, a, b * TILE:(b + 1) * TILE] = tile
            gram[t:t + 1] = tiles[t * PACK + TILE:(t + 1) * PACK, :rank]


def unpack(tiles, count, groups, rank):
    return pl.pallas_call(
        unpack_kernel,
        out_shape=[jax.ShapeDtypeStruct((count, groups, rank, BLOCK), jnp.float32),
                   jax.ShapeDtypeStruct((rank, rank), jnp.float32)],
        cost_estimate=pl.CostEstimate(flops=0, bytes_accessed=tiles.size * 20, transcendentals=0),
        compiler_params=PARAMS,
        name="unpack",
    )(tiles)


def factors_kernel(p_mean, inverse, p_factor, weights):
    p = lax.dot_general(p_mean[...], inverse[...], (((1,), (1,)), ((), ())), precision=HIGHEST,
                        preferred_element_type=jnp.float32)
    w = jnp.dot(p, inverse[...], precision=HIGHEST, preferred_element_type=jnp.float32)
    p_factor[...] = p
    weights[...] = jnp.concatenate([w, w], axis=1)


def factors(p_mean, inverse):
    rows, rank = p_mean.shape
    return pl.pallas_call(
        factors_kernel,
        out_shape=[jax.ShapeDtypeStruct((rows, rank), jnp.float32),
                   jax.ShapeDtypeStruct((rows, 2 * rank), jnp.float32)],
        cost_estimate=pl.CostEstimate(flops=4 * rows * rank * rank, bytes_accessed=20 * rows * rank, transcendentals=0),
        compiler_params=PARAMS,
        name="factors",
    )(p_mean, inverse)


def halves(value, axis):
    high = value.astype(jnp.bfloat16)
    low = (value - high.astype(jnp.float32)).astype(jnp.bfloat16)
    return jnp.concatenate([high, low], axis=axis)


def remainder(factor, s, x, a, core, gradient, error):
    chips, _, rank, _ = s.shape
    stack = halves(jnp.concatenate([s[x, a], s[x + 1, a]], axis=1), 0)
    change = jnp.dot(factor, stack, preferred_element_type=jnp.float32)
    rows = change.shape[0] // 2
    change = change[:rows] + change[rows:]
    return [
        (moment_block(gradient, error, CORES * (a * chips + x + i) + core)
         - change[:, i * BLOCK:(i + 1) * BLOCK]).astype(gradient.dtype)
        for i in range(2)]


def half_kernel(factor, s, core, gradient, error, out, blocks, done):
    chips, groups, _, _ = s.shape
    copies = []
    for a in range(groups):
        for x in range(0, chips, 2):
            blocks[a, x], blocks[a, x + 1] = remainder(factor, s, x, a, core, gradient, error)
            for i in (x, x + 1):
                start = pl.multiple_of((CORES * (a * chips + i) + core) * BLOCK, BLOCK)
                copies.append(pltpu.make_async_copy(
                    blocks.at[a, i], out.at[0, :, pl.ds(start, BLOCK)], done.at[a, i]))
                copies[-1].start()
    return copies


def near_kernel(place, weights, mine, gradient, error, out, blocks, done):
    factor = halves(weights[...], 0)
    for copy in half_kernel(factor, mine, place[0], gradient, error, out, blocks, done):
        copy.wait()


def half_scratch(s, gradient):
    chips, groups, _, _ = s.shape
    return [pltpu.VMEM((groups, chips, gradient.shape[1], BLOCK), gradient.dtype),
            pltpu.SemaphoreType.DMA((groups, chips))]


def half_cost(s, gradient):
    _, rows, cols = gradient.shape
    return pl.CostEstimate(flops=4 * rows * cols * s.shape[2], bytes_accessed=4 * rows * cols, transcendentals=0)


def update_near(place, weights, mine, gradient, error):
    return pl.pallas_call(
        near_kernel,
        in_specs=[SCALARS] + [VECTORS] * 4,
        out_specs=pl.BlockSpec(memory_space=pl.ANY),
        out_shape=jax.ShapeDtypeStruct(gradient.shape, gradient.dtype),
        scratch_shapes=half_scratch(mine, gradient),
        cost_estimate=half_cost(mine, gradient),
        compiler_params=PARAMS,
        name="update_near",
    )(place, weights, mine, gradient, error)


def far_kernel(place, weights, inverse, mine, theirs, gradient, error, near, out, right, blocks, done, held, sent):
    core, block, chip, parity = (place[i] for i in range(4))
    s = jnp.where(core == parity, mine[chip, block], theirs[chip, block])
    held[...] = jnp.dot(inverse[...], s, precision=HIGHEST, preferred_element_type=jnp.float32)
    send = pltpu.make_async_copy(held, right, sent)
    send.start()
    factor = halves(weights[...], 0)
    copies = half_kernel(factor, theirs, 1 - core, gradient, error, out, blocks, done)
    for copy in copies + [send]:
        copy.wait()


def update_far(place, weights, inverse, mine, theirs, near, gradient, error):
    rank = mine.shape[2]
    return pl.pallas_call(
        far_kernel,
        in_specs=[SCALARS] + [VECTORS] * 6 + [pl.BlockSpec(memory_space=pl.ANY)],
        out_specs=[pl.BlockSpec(memory_space=pl.ANY)] * 2,
        out_shape=[jax.ShapeDtypeStruct(gradient.shape, gradient.dtype),
                   jax.ShapeDtypeStruct((rank, BLOCK), jnp.float32)],
        input_output_aliases={7: 0},
        scratch_shapes=half_scratch(theirs, gradient) + [
            pltpu.VMEM((rank, BLOCK), jnp.float32), pltpu.SemaphoreType.DMA],
        cost_estimate=half_cost(theirs, gradient),
        compiler_params=PARAMS,
        name="update_far",
    )(place, weights, inverse, mine, theirs, gradient, error, near)


def body(gradient, error, q_prev):
    replicas = lax.axis_size("replica")
    shards = lax.axis_size("mp")
    rows, cols = gradient.shape[1:]
    rank = q_prev.shape[1]
    own = cols // replicas
    groups = own // BLOCK
    replica = lax.axis_index("replica").astype(jnp.int32)
    shard = lax.axis_index("mp").astype(jnp.int32)
    core = replica % CORES
    outer, inner = shard // replicas, shard % replicas
    chip_groups = [[c + CORES * x for x in range(replicas // CORES)] for c in range(CORES)]

    q_block = lax.ppermute(q_prev.T[None], ("replica", "mp"), [
        (r * shards + o * replicas + i, i * shards + o * replicas + r)
        for r in range(replicas) for o in range(groups) for i in range(replicas)
    ])

    keep, give = split_moment(core.reshape(1), gradient, error, own)
    give, q_block = lax.optimization_barrier((give, q_block))

    def along(value, apart):
        return lax.ppermute(value, "mp", [(j, j ^ (apart * replicas)) for j in range(shards)])
    pair = jnp.concatenate([q_block, along(q_block, 1)], axis=0)
    paired, pair = lax.optimization_barrier((keep + swap_cores(give, replicas), pair))
    parts = exchange(paired, "replica", chip_groups)
    pairs = [pair] + [along(pair, apart) for apart in (2, 4, 6)]
    mean, copies = product(outer.reshape(1), parts, pairs, replicas)

    p_mean, tiles = pack(exchange(copies, "replica"), mean, shards)
    packed = (shards, PACK, 1, BLOCK)
    tiles = exchange(tiles.reshape(packed), "mp").reshape(tiles.shape)
    tiles = exchange(total(tiles).reshape(packed), "mp").reshape(tiles.shape)
    copies, gram = unpack(tiles, replicas // CORES, groups, rank)
    mine = exchange(copies, "replica", chip_groups)

    lower = jnp.linalg.cholesky(gram)
    inverse = lax.linalg.triangular_solve(
        lower, jnp.eye(rank, dtype=jnp.float32), left_side=True, lower=True
    )
    p_factor, weights = factors(p_mean, inverse)
    mine, weights, inverse = lax.optimization_barrier((mine, weights, inverse))
    theirs = swap_cores(mine, replicas)

    place = jnp.stack([core, outer, inner // CORES, inner % CORES])
    near = update_near(place, weights, mine, gradient, error)
    new_error, right = update_far(place, weights, inverse, mine, theirs, near, gradient, error)
    return (new_error, right.T, p_factor)


def solution(mesh):
    return jax.shard_map(
        body,
        mesh=mesh,
        in_specs=(P("replica", "mp", None), P("replica", "mp", None), P("mp", None)),
        out_specs=(P("replica", "mp", None), P("mp", None), P("mp", None)),
        check_vma=False,
    )
```

```python
import jax
import jax.numpy as jnp
from jax import lax
from jax.experimental import pallas as pl
from jax.experimental.pallas import tpu as pltpu
from jax.sharding import PartitionSpec as P

HIGHEST = lax.Precision.HIGHEST
BLOCK = 128
CORES = 2
TILE = 8
PACK = 9
PARAMS = pltpu.CompilerParams(vmem_limit_bytes=16 * 2**20)


def exchange(value, axis, groups=None):
    return lax.all_to_all(value, axis, 0, 0, axis_index_groups=groups)


def swap_cores(value, replicas):
    return lax.ppermute(value, "replica", [(r, r ^ 1) for r in range(replicas)])


SCALARS = pl.BlockSpec(memory_space=pltpu.SMEM)
VECTORS = pl.BlockSpec(memory_space=pltpu.VMEM)


def moment_block(gradient, error, block):
    columns = pl.ds(pl.multiple_of(block * BLOCK, BLOCK), BLOCK)
    return gradient[0, :, columns].astype(jnp.float32) + error[0, :, columns].astype(jnp.float32)


def split_kernel(core_ref, gradient, error, keep, give):
    chips, _, own = keep.shape
    for x in range(chips):
        for out, core in ((keep, core_ref[0]), (give, 1 - core_ref[0])):
            for k in range(own // BLOCK):
                out[x, :, k * BLOCK:(k + 1) * BLOCK] = moment_block(
                    gradient, error, CORES * (k * chips + x) + core)


def split_moment(core, gradient, error, own):
    _, rows, cols = gradient.shape
    shape = jax.ShapeDtypeStruct((cols // own // CORES, rows, own), jnp.float32)
    return pl.pallas_call(
        split_kernel,
        in_specs=[SCALARS, VECTORS, VECTORS],
        out_shape=[shape, shape],
        cost_estimate=pl.CostEstimate(flops=rows * cols, bytes_accessed=8 * rows * cols, transcendentals=0),
        compiler_params=PARAMS,
        name="split_moment",
    )(core, gradient, error)


def product_kernel(outer_ref, parts, *refs):
    *pairs, mean, copies, q_list = refs
    mean[...] = (parts[0] + parts[1] + parts[2] + parts[3]) * (1.0 / copies.shape[0])
    for i, pair in enumerate(pairs):
        q_list[2 * i:2 * (i + 1)] = pair[...]
    blocks = []
    for a in range(q_list.shape[0]):
        apart = outer_ref[0] ^ a
        blocks.append(q_list[apart])
    q_own = jnp.concatenate(blocks, axis=1)
    p = lax.dot_general(mean[...], q_own, (((1,), (1,)), ((), ())), precision=HIGHEST,
                        preferred_element_type=jnp.float32)
    half = p.shape[0] // 2
    folded = jnp.concatenate([p[:half], p[half:]], axis=1)
    for r in range(copies.shape[0]):
        copies[r] = folded


def product(outer, parts, pairs, replicas):
    _, rows, own = parts.shape
    rank = pairs[0].shape[1]
    return pl.pallas_call(
        product_kernel,
        in_specs=[SCALARS, VECTORS] + [VECTORS] * len(pairs),
        out_shape=[jax.ShapeDtypeStruct((rows, own), jnp.float32),
                   jax.ShapeDtypeStruct((replicas, rows // 2, 2 * rank), jnp.float32)],
        scratch_shapes=[pltpu.VMEM((2 * len(pairs), rank, BLOCK), jnp.float32)],
        cost_estimate=pl.CostEstimate(flops=2 * rows * own * rank, bytes_accessed=4 * parts.size, transcendentals=0),
        compiler_params=PARAMS,
        name="product",
    )(outer, parts, *pairs)


def pack_kernel(p_parts, mean, p_mean, tiles):
    folded = p_parts[0]
    for r in range(1, p_parts.shape[0]):
        folded = folded + p_parts[r]
    rank = folded.shape[1] // 2
    p = jnp.concatenate([folded[:, :rank], folded[:, rank:]], axis=0)
    p_mean[...] = p
    over_rows = (((0,), (0,)), ((), ()))
    s = lax.dot_general(p, mean[...], over_rows, precision=HIGHEST, preferred_element_type=jnp.float32)
    gram = lax.dot_general(p, p, over_rows, precision=HIGHEST, preferred_element_type=jnp.float32)
    gram = jnp.concatenate([gram] * (BLOCK // rank), axis=1)
    slabs = rank // TILE
    for a in range(mean.shape[1] // BLOCK):
        for b in range(slabs):
            t = a * slabs + b
            tiles[t * PACK:t * PACK + TILE] = s[b * TILE:(b + 1) * TILE, a * BLOCK:(a + 1) * BLOCK]
            tiles[t * PACK + TILE:(t + 1) * PACK] = gram[t:t + 1]


def pack(p_parts, mean, shards):
    rows, own = mean.shape
    rank = p_parts.shape[2] // 2
    return pl.pallas_call(
        pack_kernel,
        out_shape=[jax.ShapeDtypeStruct((rows, rank), jnp.float32),
                   jax.ShapeDtypeStruct((shards * PACK, BLOCK), jnp.float32)],
        cost_estimate=pl.CostEstimate(flops=2 * rows * own * rank, bytes_accessed=8 * mean.size, transcendentals=0),
        compiler_params=PARAMS,
        name="pack",
    )(p_parts, mean)


def total_kernel(tiles, copies):
    shards = tiles.shape[0] // PACK
    parts = [tiles[t * PACK:(t + 1) * PACK] for t in range(shards)]
    while len(parts) > 1:
        parts = [parts[i] + parts[i + 1] for i in range(0, len(parts), 2)]
    for t in range(shards):
        copies[t * PACK:(t + 1) * PACK] = parts[0]


def total(tiles):
    return pl.pallas_call(
        total_kernel,
        out_shape=jax.ShapeDtypeStruct(tiles.shape, tiles.dtype),
        cost_estimate=pl.CostEstimate(flops=tiles.size, bytes_accessed=8 * tiles.size, transcendentals=0),
        compiler_params=PARAMS,
        name="total",
    )(tiles)


def unpack_kernel(tiles, copies, gram):
    count, groups, rank, _ = copies.shape
    slabs = rank // TILE
    for a in range(groups):
        for b in range(slabs):
            t = a * slabs + b
            tile = tiles[t * PACK:t * PACK + TILE]
            for x in range(count):
                copies[x, a, b * TILE:(b + 1) * TILE] = tile
            gram[t:t + 1] = tiles[t * PACK + TILE:(t + 1) * PACK, :rank]


def unpack(tiles, count, groups, rank):
    return pl.pallas_call(
        unpack_kernel,
        out_shape=[jax.ShapeDtypeStruct((count, groups, rank, BLOCK), jnp.float32),
                   jax.ShapeDtypeStruct((rank, rank), jnp.float32)],
        cost_estimate=pl.CostEstimate(flops=0, bytes_accessed=tiles.size * 20, transcendentals=0),
        compiler_params=PARAMS,
        name="unpack",
    )(tiles)


def factors_kernel(p_mean, inverse, p_factor, weights):
    p = lax.dot_general(p_mean[...], inverse[...], (((1,), (1,)), ((), ())), precision=HIGHEST,
                        preferred_element_type=jnp.float32)
    w = jnp.dot(p, inverse[...], precision=HIGHEST, preferred_element_type=jnp.float32)
    p_factor[...] = p
    weights[...] = jnp.concatenate([w, w], axis=1)


def factors(p_mean, inverse):
    rows, rank = p_mean.shape
    return pl.pallas_call(
        factors_kernel,
        out_shape=[jax.ShapeDtypeStruct((rows, rank), jnp.float32),
                   jax.ShapeDtypeStruct((rows, 2 * rank), jnp.float32)],
        cost_estimate=pl.CostEstimate(flops=4 * rows * rank * rank, bytes_accessed=20 * rows * rank, transcendentals=0),
        compiler_params=PARAMS,
        name="factors",
    )(p_mean, inverse)


def halves(value, axis):
    high = value.astype(jnp.bfloat16)
    low = (value - high.astype(jnp.float32)).astype(jnp.bfloat16)
    return jnp.concatenate([high, low], axis=axis)


def remainder(factor, s, x, a, core, gradient, error):
    chips, _, rank, _ = s.shape
    stack = halves(jnp.concatenate([s[x, a], s[x + 1, a]], axis=1), 0)
    change = jnp.dot(factor, stack, preferred_element_type=jnp.float32)
    rows = change.shape[0] // 2
    change = change[:rows] + change[rows:]
    return [
        (moment_block(gradient, error, CORES * (a * chips + x + i) + core)
         - change[:, i * BLOCK:(i + 1) * BLOCK]).astype(gradient.dtype)
        for i in range(2)]


def half_kernel(factor, s, core, gradient, error, out, blocks, done):
    chips, groups, _, _ = s.shape
    copies = []
    for a in range(groups):
        for x in range(0, chips, 2):
            blocks[a, x], blocks[a, x + 1] = remainder(factor, s, x, a, core, gradient, error)
            for i in (x, x + 1):
                start = pl.multiple_of((CORES * (a * chips + i) + core) * BLOCK, BLOCK)
                copies.append(pltpu.make_async_copy(
                    blocks.at[a, i], out.at[0, :, pl.ds(start, BLOCK)], done.at[a, i]))
                copies[-1].start()
    return copies


def near_kernel(place, weights, mine, gradient, error, out, blocks, done):
    factor = halves(weights[...], 0)
    for copy in half_kernel(factor, mine, place[0], gradient, error, out, blocks, done):
        copy.wait()


def half_scratch(s, gradient):
    chips, groups, _, _ = s.shape
    return [pltpu.VMEM((groups, chips, gradient.shape[1], BLOCK), gradient.dtype),
            pltpu.SemaphoreType.DMA((groups, chips))]


def half_cost(s, gradient):
    _, rows, cols = gradient.shape
    return pl.CostEstimate(flops=4 * rows * cols * s.shape[2], bytes_accessed=4 * rows * cols, transcendentals=0)


def update_near(place, weights, mine, gradient, error):
    return pl.pallas_call(
        near_kernel,
        in_specs=[SCALARS] + [VECTORS] * 4,
        out_specs=pl.BlockSpec(memory_space=pl.ANY),
        out_shape=jax.ShapeDtypeStruct(gradient.shape, gradient.dtype),
        scratch_shapes=half_scratch(mine, gradient),
        cost_estimate=half_cost(mine, gradient),
        compiler_params=PARAMS,
        name="update_near",
    )(place, weights, mine, gradient, error)


def far_kernel(place, weights, inverse, mine, theirs, gradient, error, near, out, right, blocks, done, held, sent):
    core, block, chip, parity = (place[i] for i in range(4))
    s = jnp.where(core == parity, mine[chip, block], theirs[chip, block])
    held[...] = jnp.dot(inverse[...], s, precision=HIGHEST, preferred_element_type=jnp.float32)
    send = pltpu.make_async_copy(held, right, sent)
    send.start()
    factor = halves(weights[...], 0)
    copies = half_kernel(factor, theirs, 1 - core, gradient, error, out, blocks, done)
    for copy in copies + [send]:
        copy.wait()


def update_far(place, weights, inverse, mine, theirs, near, gradient, error):
    rank = mine.shape[2]
    return pl.pallas_call(
        far_kernel,
        in_specs=[SCALARS] + [VECTORS] * 6 + [pl.BlockSpec(memory_space=pl.ANY)],
        out_specs=[pl.BlockSpec(memory_space=pl.ANY)] * 2,
        out_shape=[jax.ShapeDtypeStruct(gradient.shape, gradient.dtype),
                   jax.ShapeDtypeStruct((rank, BLOCK), jnp.float32)],
        input_output_aliases={7: 0},
        scratch_shapes=half_scratch(theirs, gradient) + [
            pltpu.VMEM((rank, BLOCK), jnp.float32), pltpu.SemaphoreType.DMA],
        cost_estimate=half_cost(theirs, gradient),
        compiler_params=PARAMS,
        name="update_far",
    )(place, weights, inverse, mine, theirs, gradient, error, near)


def body(gradient, error, q_prev):
    replicas = lax.axis_size("replica")
    shards = lax.axis_size("mp")
    rows, cols = gradient.shape[1:]
    rank = q_prev.shape[1]
    own = cols // replicas
    groups = own // BLOCK
    replica = lax.axis_index("replica").astype(jnp.int32)
    shard = lax.axis_index("mp").astype(jnp.int32)
    core = replica % CORES
    outer, inner = shard // replicas, shard % replicas
    chip_groups = [[c + CORES * x for x in range(replicas // CORES)] for c in range(CORES)]

    q_block = lax.ppermute(q_prev.T[None], ("replica", "mp"), [
        (r * shards + o * replicas + i, i * shards + o * replicas + r)
        for r in range(replicas) for o in range(groups) for i in range(replicas)
    ])

    keep, give = split_moment(core.reshape(1), gradient, error, own)
    give, q_block = lax.optimization_barrier((give, q_block))

    def along(value, apart):
        return lax.ppermute(value, "mp", [(j, j ^ (apart * replicas)) for j in range(shards)])
    paired, q_block = lax.optimization_barrier((keep + swap_cores(give, replicas), q_block))
    parts = exchange(paired, "replica", chip_groups)
    pair = jnp.concatenate([q_block, along(q_block, 1)], axis=0)
    pairs = [pair] + [along(pair, apart) for apart in (2, 4, 6)]
    mean, copies = product(outer.reshape(1), parts, pairs, replicas)

    p_mean, tiles = pack(exchange(copies, "replica"), mean, shards)
    packed = (shards, PACK, 1, BLOCK)
    tiles = exchange(tiles.reshape(packed), "mp").reshape(tiles.shape)
    tiles = exchange(total(tiles).reshape(packed), "mp").reshape(tiles.shape)
    copies, gram = unpack(tiles, replicas // CORES, groups, rank)
    mine = exchange(copies, "replica", chip_groups)

    lower = jnp.linalg.cholesky(gram)
    inverse = lax.linalg.triangular_solve(
        lower, jnp.eye(rank, dtype=jnp.float32), left_side=True, lower=True
    )
    p_factor, weights = factors(p_mean, inverse)
    mine, weights, inverse = lax.optimization_barrier((mine, weights, inverse))
    theirs = swap_cores(mine, replicas)

    place = jnp.stack([core, outer, inner // CORES, inner % CORES])
    near = update_near(place, weights, mine, gradient, error)
    new_error, right = update_far(place, weights, inverse, mine, theirs, near, gradient, error)
    return (new_error, right.T, p_factor)


def solution(mesh):
    return jax.shard_map(
        body,
        mesh=mesh,
        in_specs=(P("replica", "mp", None), P("replica", "mp", None), P("mp", None)),
        out_specs=(P("replica", "mp", None), P("mp", None), P("mp", None)),
        check_vma=False,
    )
```
